32 devices in a mesh: gx: 16 (over z, y, x), gy: 2 (over core).
Axes of the slice: x: 2, y: 2, z: 4, core: 2. Of those that a mesh axis runs over, the one named last changes fastest.
Arguments:
- rhs: float32 [16, 2, 128, 128], P('gx', 'gy'), may hold values from -57 to 57
- face_rows: int32 [16, 2, 4, 128], P('gx', 'gy'), may hold values from 0 to 127
- margin_weight: float32 [16, 2, 4, 128], P('gx', 'gy'), may hold values from 0.2 to 1
- local_blocks: bfloat16 [16, 2, 1, 128, 128], P('gx', 'gy'), may hold values from -0.4 to 4.4
- subdomain_inverse: bfloat16 [16, 2, 128, 640], P('gx', 'gy'), may hold values from -0.4 to 1.8
- coarse_basis: bfloat16 [16, 2, 128, 32], P('gx', 'gy'), may hold values from -0.5 to 0.5
- coarse_inverse: bfloat16 [16, 2, 32, 1024], P('gx', 'gy'), may hold values from -0.390625 to 0.390625
- coarse_map: int32 [32], replicated, may hold values from 0 to 31, each once
Outputs:
- solution: float32 [16, 2, 128, 128], P('gx', 'gy')
- relative_residual: float32 [128], replicated
The draws below stay inside these ranges and needn't reach their ends.
Inputs may be any that keep to these rules, and one draw needn't show every extreme that they name: `face_rows`: rows of the subdomain, repeats possible. `coarse_map`: every position once.
All inputs are finite; a program needn't handle non-finite values.
Results may differ from the reference program's by a relative error of at most 0.004.
Values may be sent and summed in bfloat16 or wider, within the bound.
A program may use at most 64 MiB of HBM per device.

```python
import math
import jax
import jax.numpy as jnp
from jax import lax

NLOC = 128
NRHS = 128
H = 128
BK = 128
NCV = 32
NB = 1
NE = 640
NSUB = 32
NCOARSE = 1024
N_GX = 16
N_GY = 2


def draw_rhs(key, part):
    key_base, key_rows = jax.random.split(key, 2)
    full_shape = (N_GX, N_GY, NLOC, NRHS)
    row_scale = jnp.exp(math.log(10.0) * jax.random.uniform(key_rows, (N_GX, N_GY, NLOC, 1), jnp.float32))
    growth = 1.0 + 2.0 * jnp.arange(N_GX, dtype=jnp.float32).reshape(N_GX, 1, 1, 1) / max(N_GX - 1, 1)
    standard = jnp.clip(jax.random.normal(key_base, full_shape, jnp.float32), -5.0, 5.0)
    return (standard * row_scale * growth / 8.0).astype(jnp.float32)


def draw_local_blocks(key, part):
    key_diag, key_noise = jax.random.split(key)
    diagonal = jax.random.uniform(key_diag, (N_GX, N_GY, NB, BK, 1), jnp.float32, 2.0, 4.0)
    noise = jnp.clip(jax.random.normal(key_noise, (N_GX, N_GY, NB, BK, BK), jnp.float32), -5.0, 5.0)
    return (jnp.eye(BK, dtype=jnp.float32) * diagonal + noise * (0.8 / math.sqrt(BK))).astype(jnp.bfloat16)


def draw_subdomain_inverse(key, part):
    key_diag, key_noise = jax.random.split(key)
    diagonal = jax.random.uniform(key_diag, (N_GX, N_GY, NLOC, 1), jnp.float32, 0.6, 1.4)
    noise = jnp.clip(jax.random.normal(key_noise, (N_GX, N_GY, NLOC, NE), jnp.float32), -5.0, 5.0)
    return (jnp.eye(NLOC, NE, dtype=jnp.float32) * diagonal + noise * (0.8 / math.sqrt(NE))).astype(jnp.bfloat16)


def draw_coarse_inverse(key, part):
    noise = jnp.clip(jax.random.normal(key, (N_GX, N_GY, NCV, NCOARSE), jnp.float32), -5.0, 5.0)
    return (noise * (2.5 / math.sqrt(NCOARSE))).astype(jnp.bfloat16)


def plant(array, own_key, smallest, largest):
    longest = array.shape.index(max(array.shape))
    spots = []
    for shift in (0, 1):
        where = [jax.random.randint(jax.random.fold_in(own_key, axis), (), 0, length) for axis, length in enumerate(array.shape)]
        where[longest] = (where[longest] + shift) % array.shape[longest]
        spots.append(tuple(where))
    return array.at[spots[0]].set(smallest).at[spots[1]].set(largest)


def levels(own_key, shape, pieces, smallest, largest):
    factor_of, own = 1.0, jax.random.fold_in(own_key, 6)
    for position, parts in pieces:
        heights = jnp.exp(jax.random.uniform(jax.random.fold_in(own, position), (parts,), jnp.float32, smallest / len(pieces), largest / len(pieces)))
        factor_of = factor_of * jnp.repeat(heights, shape[position] // parts).reshape([-1 if axis == position else 1 for axis in range(len(shape))])
    return factor_of


def centred(stream_key, shape, deviation, most, shards=(), held_as=jnp.bfloat16):
    array = deviation * jax.random.normal(stream_key, shape, jnp.float32)
    if shards:
        array = array * levels(stream_key, shape, shards, -0.22, 0.18)
    return jnp.clip(array, -most, most).astype(held_as)


def setup_inputs(seed: int = 0) -> dict:
    key_list = jax.random.split(jax.random.key(seed), 9)
    rhs = draw_rhs(jax.random.fold_in(key_list[8], 71), 0)
    face_rows = plant(jax.random.randint(key_list[1], (N_GX, N_GY, 4, H), 0, NLOC), jax.random.fold_in(key_list[1], 1), 0, NLOC - 1).astype(jnp.int32)
    margin_weight = jnp.clip(jnp.exp(math.log(1.0) - 1.609438 * jax.random.uniform(key_list[2], (N_GX, N_GY, 4, H), jnp.float32) ** levels(key_list[2], (N_GX, N_GY, 4, H), ((0, 16), (1, 2)), -0.2, 0.2)), 0.2, 1.0)
    local_blocks = draw_local_blocks(jax.random.fold_in(key_list[8], 71), 0)
    subdomain_inverse = draw_subdomain_inverse(jax.random.fold_in(key_list[8], 71), 0)
    coarse_basis = centred(key_list[5], (N_GX, N_GY, NLOC, NCV), NLOC ** -0.5, 0.5, ((0, 16), (1, 2)))
    coarse_inverse = draw_coarse_inverse(jax.random.fold_in(key_list[8], 71), 0)
    coarse_map = jax.random.permutation(key_list[7], NSUB).astype(jnp.int32)
    return dict(rhs=rhs, face_rows=face_rows, margin_weight=margin_weight, local_blocks=local_blocks, subdomain_inverse=subdomain_inverse, coarse_basis=coarse_basis, coarse_inverse=coarse_inverse, coarse_map=coarse_map)


EPSILON = 1e-06

def least_squares(scale_norm, first_dot, first_norm, cross_dot, second_dot, second_norm):
    radius_one = jnp.sqrt(first_dot * first_dot + first_norm * first_norm)
    cosine_one = first_dot / radius_one
    sine_one = first_norm / radius_one
    upper_entry = cosine_one * cross_dot + sine_one * second_dot
    lower_entry = cosine_one * second_dot - sine_one * cross_dot
    radius_two = jnp.sqrt(lower_entry * lower_entry + second_norm * second_norm)
    cosine_two = lower_entry / radius_two
    sine_two = second_norm / radius_two
    weight_two = -cosine_two * sine_one * scale_norm / radius_two
    weight_one = (cosine_one * scale_norm - upper_entry * weight_two) / radius_one
    return (weight_one, weight_two, sine_one * sine_two)

def neighbour_margin(rounded, face_rows):
    face_packs = jax.vmap(jax.vmap(lambda subdomain_field, margin_rows: subdomain_field[margin_rows]))(rounded, face_rows)
    below_first = jnp.concatenate([jnp.zeros_like(face_packs[:1, :, 1]), face_packs[:-1, :, 1]], axis=0)
    above_first = jnp.concatenate([face_packs[1:, :, 0], jnp.zeros_like(face_packs[:1, :, 0])], axis=0)
    below_second = jnp.concatenate([jnp.zeros_like(face_packs[:, :1, 3]), face_packs[:, :-1, 3]], axis=1)
    above_second = jnp.concatenate([face_packs[:, 1:, 2], jnp.zeros_like(face_packs[:, :1, 2])], axis=1)
    return jnp.stack([below_first, above_first, below_second, above_second], axis=2)

def precondition(vector, face_rows, subdomain_inverse, coarse_basis, coarse_inverse, coarse_map):
    rounded = vector.astype(jnp.bfloat16)
    margin = neighbour_margin(rounded, face_rows).reshape(N_GX, N_GY, 4 * H, NRHS)
    extended = jnp.concatenate([rounded, margin], axis=2).reshape(NSUB, NE, NRHS)
    inverse_rows = subdomain_inverse.reshape(NSUB, NLOC, NE)
    local_part = lax.map(lambda operands: jnp.dot(operands[0], operands[1], preferred_element_type=jnp.float32), (inverse_rows, extended))
    basis = coarse_basis.reshape(NSUB, NLOC, NCV)
    flat_field = rounded.reshape(NSUB, NLOC, NRHS)
    residual = lax.map(lambda operands: jnp.dot(operands[0].T, operands[1], preferred_element_type=jnp.float32), (basis, flat_field)).astype(jnp.bfloat16)
    placed = jnp.zeros((NSUB, NCV, NRHS), jnp.bfloat16).at[coarse_map].set(residual).reshape(NCOARSE, NRHS)
    solved = jnp.dot(coarse_inverse.reshape(NCOARSE, NCOARSE), placed, preferred_element_type=jnp.float32).astype(jnp.bfloat16).reshape(NSUB, NCV, NRHS)
    prolonged = lax.map(lambda operands: jnp.dot(operands[0], operands[1], preferred_element_type=jnp.float32), (basis, solved))
    return (local_part + prolonged).reshape(N_GX, N_GY, NLOC, NRHS)

def apply_operator(vector, face_rows, margin_weight, local_blocks):
    rounded = vector.astype(jnp.bfloat16)
    margin = neighbour_margin(rounded, face_rows).astype(jnp.float32)
    shaped = rounded.reshape(N_GX, N_GY, NB, BK, NRHS).astype(jnp.float32)
    own_part = jnp.einsum('xybrc,xybcn->xybrn', local_blocks.astype(jnp.float32), shaped, precision=lax.Precision.HIGHEST).reshape(N_GX, N_GY, NLOC, NRHS)
    weighted = margin_weight[..., None] * margin

    def spread(margin_rows, margin_values):
        return jnp.zeros((NLOC, NRHS), jnp.float32).at[margin_rows.reshape(-1)].add(margin_values.reshape(4 * H, NRHS))
    coupling = jax.vmap(jax.vmap(spread))(face_rows, weighted)
    return own_part - coupling

def column_sum(left_field, right_field):
    return lax.optimization_barrier(jnp.sum(left_field * right_field, axis=(0, 1, 2)))

def reference(rhs, face_rows, margin_weight, local_blocks, subdomain_inverse, coarse_basis, coarse_inverse, coarse_map):
    scale_norm = jnp.sqrt(column_sum(rhs, rhs) + EPSILON)
    krylov_one = rhs / scale_norm
    precond_one = precondition(krylov_one, face_rows, subdomain_inverse, coarse_basis, coarse_inverse, coarse_map)
    applied = apply_operator(precond_one, face_rows, margin_weight, local_blocks)
    first_dot = column_sum(applied, krylov_one)
    remainder = applied - first_dot * krylov_one
    first_norm = jnp.sqrt(column_sum(remainder, remainder) + EPSILON)
    krylov_two = remainder / first_norm
    precond_two = precondition(krylov_two, face_rows, subdomain_inverse, coarse_basis, coarse_inverse, coarse_map)
    applied = apply_operator(precond_two, face_rows, margin_weight, local_blocks)
    cross_dot = column_sum(applied, krylov_one)
    second_dot = column_sum(applied, krylov_two)
    remainder = applied - cross_dot * krylov_one - second_dot * krylov_two
    second_norm = jnp.sqrt(column_sum(remainder, remainder) + EPSILON)
    weight_one, weight_two, relative = least_squares(scale_norm, first_dot, first_norm, cross_dot, second_dot, second_norm)
    solution = weight_one * precond_one + weight_two * precond_two
    return (solution, relative)
```

```python
import functools

import jax
import jax.numpy as jnp
from jax import lax
from jax.experimental import pallas as pl
from jax.experimental.pallas import tpu as pltpu
from jax.sharding import PartitionSpec as P

EPSILON = 1e-06
MESH = pl.DeviceIdType.MESH
F32 = jnp.float32
BF16 = jnp.bfloat16
LANES = 128


def least_squares(scale_norm, first_dot, first_norm, cross_dot, second_dot, second_norm):
    radius_one = jnp.sqrt(first_dot * first_dot + first_norm * first_norm)
    cosine_one = first_dot / radius_one
    sine_one = first_norm / radius_one
    upper_entry = cosine_one * cross_dot + sine_one * second_dot
    lower_entry = cosine_one * second_dot - sine_one * cross_dot
    radius_two = jnp.sqrt(lower_entry * lower_entry + second_norm * second_norm)
    cosine_two = lower_entry / radius_two
    sine_two = second_norm / radius_two
    weight_two = -cosine_two * sine_one * scale_norm / radius_two
    weight_one = (cosine_one * scale_norm - upper_entry * weight_two) / radius_one
    return (weight_one, weight_two, sine_one * sine_two)


def dot(left, right):
    return jnp.dot(left, right, preferred_element_type=F32)


def repeat(first, last, body):
    if last - first <= 8:
        for index in range(first, last):
            body(index)
    else:
        lax.fori_loop(first, last, lambda index, carry: (body(index), carry)[1], 0)


def column_sum(values):
    return jnp.sum(values, axis=0, keepdims=True)


def kernel(
    n_gx,
    n_gy,
    plane,
    rhs_ref,
    rows_ref,
    weight_ref,
    block_ref,
    inverse_ref,
    basis_ref,
    coarse_ref,
    map_ref,
    out_ref,
    relative_ref,
    coarse_t,
    pieces,
    solver,
    select,
    spread,
    basis_t,
    packs,
    margins,
    gathered,
    partial,
    received,
    line_sums,
    plane_sums,
    pieces_sem,
    margin_send,
    margin_recv,
    gather_sem,
    partial_sem,
    line_sem,
    plane_sem,
):
    i = lax.axis_index("gx")
    j = lax.axis_index("gy")
    n_line = n_gx // plane
    n_plane = plane * n_gy
    line = i // plane
    spot = (i % plane) * n_gy + j
    owned, columns = rhs_ref.shape
    width = basis_ref.shape[1]

    def line_device(slot):
        return (slot * plane + i % plane, j)

    def plane_device(slot):
        return (line * plane + slot // n_gy, slot % n_gy)

    faces = (
        ((i - 1, j), i > 0, 1),
        ((i + 1, j), i < n_gx - 1, 0),
        ((i, j - 1), j > 0, 3),
        ((i, j + 1), j < n_gy - 1, 2),
    )

    for face, (_, present, _) in enumerate(faces):

        @pl.when(jnp.logical_not(present))
        def _():
            for exchange in range(margins.shape[0]):
                margins[exchange, face] = jnp.zeros(margins.shape[2:], BF16)

    barrier = pltpu.get_barrier_semaphore()

    def greet(device):
        pl.semaphore_signal(barrier, inc=1, device_id=device, device_id_type=MESH)

    repeat(1, n_line, lambda step: greet(line_device((line + step) % n_line)))
    repeat(1, n_plane, lambda step: greet(plane_device((spot + step) % n_plane)))
    cross_down = jnp.logical_and(i % plane == 0, i > 0)
    cross_up = jnp.logical_and(i % plane == plane - 1, i < n_gx - 1)
    if plane > 1:

        @pl.when(cross_down)
        def _():
            greet((i - 1, j))

        @pl.when(cross_up)
        def _():
            greet((i + 1, j))

    right_side = rhs_ref[...]
    square_sum = column_sum(right_side * right_side)

    peers = n_line + n_plane - 2
    if plane > 1:
        peers += cross_down.astype(jnp.int32) + cross_up.astype(jnp.int32)
    pl.semaphore_wait(barrier, peers)

    def start_copy(source, target, sends, recvs, device):
        pltpu.make_async_remote_copy(
            src_ref=source,
            dst_ref=target,
            send_sem=sends,
            recv_sem=recvs,
            device_id=device,
            device_id_type=MESH,
        ).start()

    def wait_bytes(ref, sem):
        pltpu.make_async_copy(ref, ref, sem).wait()

    def line_gather(slots, sems):
        def send(step):
            device = line_device((line + step) % n_line)
            start_copy(slots.at[line], slots.at[line], sems.at[0], sems.at[1], device)

        repeat(1, n_line, send)

    def plane_gather(slots, sems):
        def send(step):
            device = plane_device((spot + step) % n_plane)
            start_copy(slots.at[spot], slots.at[spot], sems.at[0], sems.at[1], device)

        repeat(1, n_plane, send)

    def plane_scatter(sources, slots, sems):
        def send(step):
            other = (spot + step) % n_plane
            start_copy(
                sources.at[other], slots.at[spot], sems.at[0], sems.at[1], plane_device(other)
            )

        repeat(1, n_plane, send)

    def wait_line(slots, sems, which):
        if n_line > 1:
            wait_bytes(slots.at[pl.ds(0, n_line - 1)], sems.at[which])

    def wait_plane(slots, sems, which):
        if n_plane > 1:
            wait_bytes(slots.at[pl.ds(0, n_plane - 1)], sems.at[which])

    def start_sums(which, sums):
        rest = jnp.zeros((8 - len(sums), columns), F32)
        line_sums[which, line] = jnp.concatenate(list(sums) + [rest], axis=0)
        line_gather(line_sums.at[which], line_sem.at[which])

    def finish_sums(which, count):
        wait_line(line_sums.at[which], line_sem.at[which], 1)
        plane_sums[which, spot] = jnp.sum(line_sums[which], axis=0)
        plane_gather(plane_sums.at[which], plane_sem.at[which])
        wait_plane(plane_sums.at[which], plane_sem.at[which], 1)
        total = jnp.sum(plane_sums[which], axis=0)
        return [total[row : row + 1, :] for row in range(count)]

    start_sums(0, [square_sum])

    row_ids = lax.broadcasted_iota(jnp.int32, (owned, rows_ref.shape[1]), 0)
    for face in range(4):
        hit = row_ids == rows_ref[face : face + 1, :]
        one = jnp.where(hit, 1.0, 0.0).astype(F32)
        select[face] = one.T.astype(BF16)
        weights = jnp.where(hit, weight_ref[face : face + 1, :], 0.0)
        high = weights.astype(BF16)
        spread[0, face] = high
        spread[1, face] = (weights - high.astype(F32)).astype(BF16)
    basis_t[...] = basis_ref[...].astype(F32).T.astype(BF16)

    [beta_square] = finish_sums(0, 1)
    beta = jnp.sqrt(beta_square + EPSILON)

    def turn(chunk):
        start = chunk * LANES
        if not isinstance(start, int):
            start = pl.multiple_of(start, LANES)
        turned = coarse_ref[:, pl.ds(start, LANES)].astype(F32).T
        count = LANES // width
        coarse_t[pl.ds(chunk * count, count)] = turned.reshape(count, width, width)

    def arrange(member):
        parts = []
        for other_line in range(n_line):
            parts.append(coarse_t[map_ref[other_line * n_plane + member]])
        pieces[member] = jnp.concatenate(parts, axis=0).T.astype(BF16)

    def send_pieces():
        repeat(0, coarse_ref.shape[1] // LANES, turn)
        repeat(0, n_plane, arrange)
        plane_scatter(pieces, solver, pieces_sem)
        solver[spot] = pieces[spot]

    def start_margins(exchange, rounded):
        packs[exchange] = dot(
            select[...].reshape(-1, owned), rounded
        ).astype(BF16).reshape(packs.shape[1:])
        for face, (device, present, block) in enumerate(faces):

            @pl.when(present)
            def _():
                start_copy(
                    packs.at[exchange, face],
                    margins.at[exchange, block],
                    margin_send.at[exchange, face],
                    margin_recv.at[exchange, block],
                    device,
                )

    def wait_margins(exchange):
        for face, (_, present, _) in enumerate(faces):

            @pl.when(present)
            def _():
                wait_bytes(margins.at[exchange, face], margin_recv.at[exchange, face])

    def precondition(turn_index, vector):
        exchange = 2 * turn_index
        rounded = vector.astype(BF16)
        residual = dot(basis_t[...], rounded).astype(BF16)
        gathered[turn_index, line] = residual
        line_gather(gathered.at[turn_index], gather_sem.at[turn_index])
        start_margins(exchange, rounded)
        if turn_index == 0:
            send_pieces()
        local = dot(inverse_ref[:, :owned], rounded)
        if turn_index == 0:
            wait_plane(solver, pieces_sem, 1)
        wait_line(gathered.at[turn_index], gather_sem.at[turn_index], 1)
        partial[turn_index] = dot(
            solver[...].reshape(n_plane * width, n_line * width),
            gathered[turn_index].reshape(n_line * width, columns),
        ).reshape(n_plane, width, columns)
        plane_scatter(
            partial.at[turn_index], received.at[turn_index], partial_sem.at[turn_index]
        )
        received[turn_index, spot] = partial[turn_index, spot]
        wait_margins(exchange)
        local += dot(inverse_ref[:, owned:], margins[exchange].reshape(-1, columns))
        wait_plane(received.at[turn_index], partial_sem.at[turn_index], 1)
        solved = jnp.sum(received[turn_index], axis=0).astype(BF16)
        return local + dot(basis_ref[...], solved)

    def apply_operator(turn_index, vector):
        exchange = 2 * turn_index + 1
        rounded = vector.astype(BF16)
        start_margins(exchange, rounded)
        size = block_ref.shape[1]
        own = [
            dot(block_ref[block], rounded[block * size : (block + 1) * size])
            for block in range(block_ref.shape[0])
        ]
        own = own[0] if len(own) == 1 else jnp.concatenate(own, axis=0)
        wait_margins(exchange)
        for face in range(4):
            margin = margins[exchange, face]
            own -= dot(spread[0, face], margin) + dot(spread[1, face], margin)
        return own

    krylov_one = right_side / beta
    precond_one = precondition(0, krylov_one)
    applied = apply_operator(0, precond_one)
    start_sums(
        1,
        [
            column_sum(applied * krylov_one),
            column_sum(applied * applied),
            column_sum(krylov_one * krylov_one),
        ],
    )
    first_dot, applied_square, one_one = finish_sums(1, 3)
    remainder_square = applied_square + first_dot * first_dot * (one_one - 2.0)
    first_norm = jnp.sqrt(jnp.maximum(remainder_square, 0.0) + EPSILON)
    krylov_two = (applied - first_dot * krylov_one) / first_norm

    precond_two = precondition(1, krylov_two)
    applied = apply_operator(1, precond_two)
    start_sums(
        2,
        [
            column_sum(applied * krylov_one),
            column_sum(applied * krylov_two),
            column_sum(applied * applied),
            column_sum(krylov_one * krylov_two),
            column_sum(krylov_two * krylov_two),
        ],
    )
    cross_dot, second_dot, applied_square, one_two, two_two = finish_sums(2, 5)
    remainder_square = (
        applied_square
        + cross_dot * cross_dot * (one_one - 2.0)
        + second_dot * second_dot * (two_two - 2.0)
        + 2.0 * cross_dot * second_dot * one_two
    )
    second_norm = jnp.sqrt(jnp.maximum(remainder_square, 0.0) + EPSILON)
    weight_one, weight_two, relative = least_squares(
        beta, first_dot, first_norm, cross_dot, second_dot, second_norm
    )
    out_ref[...] = weight_one * precond_one + weight_two * precond_two
    relative_ref[...] = relative

    for which in range(3):
        wait_line(line_sums.at[which], line_sem.at[which], 0)
        wait_plane(plane_sums.at[which], plane_sem.at[which], 0)
    wait_plane(solver, pieces_sem, 0)
    for turn_index in range(2):
        wait_line(gathered.at[turn_index], gather_sem.at[turn_index], 0)
        wait_plane(received.at[turn_index], partial_sem.at[turn_index], 0)
    for exchange in range(4):
        for face, (_, present, _) in enumerate(faces):

            @pl.when(present)
            def _():
                wait_bytes(packs.at[exchange, face], margin_send.at[exchange, face])


def on_device(
    n_gx,
    n_gy,
    rhs,
    face_rows,
    margin_weight,
    local_blocks,
    subdomain_inverse,
    coarse_basis,
    coarse_inverse,
    coarse_map,
):
    plane = 4 if n_gx % 4 == 0 else 1
    n_line, n_plane = n_gx // plane, plane * n_gy
    owned, columns = rhs.shape[2:]
    margin_rows = face_rows.shape[3]
    width = coarse_basis.shape[3]
    n_coarse = coarse_inverse.shape[3]
    vmem = pl.BlockSpec(memory_space=pltpu.VMEM)
    dma = pltpu.SemaphoreType.DMA
    result, relative = pl.pallas_call(
        functools.partial(kernel, n_gx, n_gy, plane),
        out_shape=(
            jax.ShapeDtypeStruct((owned, columns), F32),
            jax.ShapeDtypeStruct((1, columns), F32),
        ),
        in_specs=[vmem] * 7 + [pl.BlockSpec(memory_space=pltpu.SMEM)],
        out_specs=(vmem, vmem),
        scratch_shapes=[
            pltpu.VMEM((n_coarse // width, width, width), F32),
            pltpu.VMEM((n_plane, width, n_line * width), BF16),
            pltpu.VMEM((n_plane, width, n_line * width), BF16),
            pltpu.VMEM((4, margin_rows, owned), BF16),
            pltpu.VMEM((2, 4, owned, margin_rows), BF16),
            pltpu.VMEM((width, owned), BF16),
            pltpu.VMEM((4, 4, margin_rows, columns), BF16),
            pltpu.VMEM((4, 4, margin_rows, columns), BF16),
            pltpu.VMEM((2, n_line, width, columns), BF16),
            pltpu.VMEM((2, n_plane, width, columns), F32),
            pltpu.VMEM((2, n_plane, width, columns), F32),
            pltpu.VMEM((3, n_line, 8, columns), F32),
            pltpu.VMEM((3, n_plane, 8, columns), F32),
            dma((2,)),
            dma((4, 4)),
            dma((4, 4)),
            dma((2, 2)),
            dma((2, 2)),
            dma((3, 2)),
            dma((3, 2)),
        ],
        compiler_params=pltpu.CompilerParams(
            collective_id=0, has_side_effects=True, vmem_limit_bytes=40 * 1024 * 1024
        ),
    )(
        rhs[0, 0],
        face_rows[0, 0],
        margin_weight[0, 0],
        local_blocks[0, 0],
        subdomain_inverse[0, 0],
        coarse_basis[0, 0],
        coarse_inverse[0, 0],
        coarse_map,
    )
    return (result[None, None], relative[0])


def solution(mesh):
    return jax.shard_map(
        functools.partial(on_device, mesh.shape["gx"], mesh.shape["gy"]),
        mesh=mesh,
        in_specs=(
            P("gx", "gy", None, None),
            P("gx", "gy", None, None),
            P("gx", "gy", None, None),
            P("gx", "gy", None, None, None),
            P("gx", "gy", None, None),
            P("gx", "gy", None, None),
            P("gx", "gy", None, None),
            P(),
        ),
        out_specs=(P("gx", "gy", None, None), P()),
        check_vma=False,
    )
```

```python
import functools

import jax
import jax.numpy as jnp
from jax import lax
from jax.experimental import pallas as pl
from jax.experimental.pallas import tpu as pltpu
from jax.sharding import PartitionSpec as P

EPSILON = 1e-06
MESH = pl.DeviceIdType.MESH
F32 = jnp.float32
BF16 = jnp.bfloat16
LANES = 128


def least_squares(scale_norm, first_dot, first_norm, cross_dot, second_dot, second_norm):
    radius_one = jnp.sqrt(first_dot * first_dot + first_norm * first_norm)
    cosine_one = first_dot / radius_one
    sine_one = first_norm / radius_one
    upper_entry = cosine_one * cross_dot + sine_one * second_dot
    lower_entry = cosine_one * second_dot - sine_one * cross_dot
    radius_two = jnp.sqrt(lower_entry * lower_entry + second_norm * second_norm)
    cosine_two = lower_entry / radius_two
    sine_two = second_norm / radius_two
    weight_two = -cosine_two * sine_one * scale_norm / radius_two
    weight_one = (cosine_one * scale_norm - upper_entry * weight_two) / radius_one
    return (weight_one, weight_two, sine_one * sine_two)


def dot(left, right):
    return jnp.dot(left, right, preferred_element_type=F32)


def repeat(first, last, body):
    if last - first <= 8:
        for index in range(first, last):
            body(index)
    else:
        lax.fori_loop(first, last, lambda index, carry: (body(index), carry)[1], 0)


def column_sum(values):
    return jnp.sum(values, axis=0, keepdims=True)


def halves(values):
    high = values.astype(BF16)
    low = (values - high.astype(F32)).astype(BF16)
    return jnp.concatenate([high, low], axis=1)


def joined(values):
    columns = values.shape[1] // 2
    return values[:, :columns] + values[:, columns:]


def kernel(
    n_gx,
    n_gy,
    plane,
    rhs_hbm,
    rows_hbm,
    weight_hbm,
    block_hbm,
    inverse_hbm,
    basis_t_hbm,
    coarse_hbm,
    map_hbm,
    out_ref,
    relative_ref,
    rhs_ref,
    rows_ref,
    weight_ref,
    block_ref,
    inverse_ref,
    basis_t,
    coarse_ref,
    map_ref,
    coarse_t,
    pieces,
    solver,
    select,
    spread,
    basis_ref,
    packs,
    margins,
    gathered,
    partial,
    received,
    line_sums,
    plane_sums,
    operand_sem,
    pieces_sem,
    margin_send,
    margin_recv,
    gather_sem,
    partial_sem,
    line_sem,
    plane_sem,
):
    i = lax.axis_index("gx")
    j = lax.axis_index("gy")
    n_line = n_gx // plane
    n_plane = plane * n_gy
    line = i // plane
    spot = (i % plane) * n_gy + j
    owned, columns = rhs_ref.shape
    width = basis_ref.shape[1]

    def line_device(slot):
        return (slot * plane + i % plane, j)

    def plane_device(slot):
        return (line * plane + slot // n_gy, slot % n_gy)

    barrier = pltpu.get_barrier_semaphore()

    def greet(device):
        pl.semaphore_signal(barrier, inc=1, device_id=device, device_id_type=MESH)

    repeat(1, n_line, lambda step: greet(line_device((line + step) % n_line)))
    repeat(1, n_plane, lambda step: greet(plane_device((spot + step) % n_plane)))
    cross_down = jnp.logical_and(i % plane == 0, i > 0)
    cross_up = jnp.logical_and(i % plane == plane - 1, i < n_gx - 1)
    peers = n_line + n_plane - 2
    if plane > 1:
        peers += cross_down.astype(jnp.int32) + cross_up.astype(jnp.int32)

        @pl.when(cross_down)
        def _():
            greet((i - 1, j))

        @pl.when(cross_up)
        def _():
            greet((i + 1, j))

    operands = {}
    for index, (name, source, target) in enumerate(
        (
            ("coarse", coarse_hbm, coarse_ref),
            ("map", map_hbm, map_ref),
            ("rhs", rhs_hbm, rhs_ref),
            ("basis", basis_t_hbm, basis_t),
            ("rows", rows_hbm, rows_ref),
            ("weight", weight_hbm, weight_ref),
            ("inverse", inverse_hbm, inverse_ref),
            ("block", block_hbm, block_ref),
        )
    ):
        operands[name] = pltpu.make_async_copy(source, target, operand_sem.at[index])
        operands[name].start()

    faces = (
        ((i - 1, j), i > 0, 1),
        ((i + 1, j), i < n_gx - 1, 0),
        ((i, j - 1), j > 0, 3),
        ((i, j + 1), j < n_gy - 1, 2),
    )

    for face, (_, present, _) in enumerate(faces):

        @pl.when(jnp.logical_not(present))
        def _():
            for exchange in range(margins.shape[0]):
                margins[exchange, face] = jnp.zeros(margins.shape[2:], BF16)

    def start_copy(source, target, sends, recvs, device):
        pltpu.make_async_remote_copy(
            src_ref=source,
            dst_ref=target,
            send_sem=sends,
            recv_sem=recvs,
            device_id=device,
            device_id_type=MESH,
        ).start()

    def wait_bytes(ref, sem):
        pltpu.make_async_copy(ref, ref, sem).wait()

    def line_gather(slots, sems):
        def send(step):
            device = line_device((line + step) % n_line)
            start_copy(slots.at[line], slots.at[line], sems.at[0], sems.at[1], device)

        repeat(1, n_line, send)

    def plane_gather(slots, sems):
        def send(step):
            device = plane_device((spot + step) % n_plane)
            start_copy(slots.at[spot], slots.at[spot], sems.at[0], sems.at[1], device)

        repeat(1, n_plane, send)

    def plane_scatter(sources, slots, sems):
        def send(step):
            other = (spot + step) % n_plane
            start_copy(
                sources.at[other], slots.at[spot], sems.at[0], sems.at[1], plane_device(other)
            )

        repeat(1, n_plane, send)

    def wait_line(slots, sems, which):
        if n_line > 1:
            wait_bytes(slots.at[pl.ds(0, n_line - 1)], sems.at[which])

    def wait_plane(slots, sems, which):
        if n_plane > 1:
            wait_bytes(slots.at[pl.ds(0, n_plane - 1)], sems.at[which])

    def tile_of(sums):
        rest = jnp.zeros((8 - len(sums), columns), F32)
        return jnp.concatenate(list(sums) + [rest], axis=0)

    def turn(chunk):
        start = chunk * LANES
        if not isinstance(start, int):
            start = pl.multiple_of(start, LANES)
        turned = coarse_ref[:, pl.ds(start, LANES)].astype(F32).T
        count = LANES // width
        coarse_t[pl.ds(chunk * count, count)] = turned.reshape(count, width, width)

    def arrange(member):
        parts = []
        for other_line in range(n_line):
            parts.append(coarse_t[map_ref[other_line * n_plane + member]])
        pieces[member] = jnp.concatenate(parts, axis=0).T.astype(BF16)

    def make_packs(exchange, rounded):
        packs[exchange] = (
            dot(select[...].reshape(-1, owned), rounded)
            .astype(BF16)
            .reshape(packs.shape[1:])
        )

    def send_packs(exchange):
        for face, (device, present, block) in enumerate(faces):

            @pl.when(present)
            def _():
                start_copy(
                    packs.at[exchange, face],
                    margins.at[exchange, block],
                    margin_send.at[exchange, face],
                    margin_recv.at[exchange, block],
                    device,
                )

    def wait_margins(exchange):
        for face, (_, present, _) in enumerate(faces):

            @pl.when(present)
            def _():
                wait_bytes(margins.at[exchange, face], margin_recv.at[exchange, face])

    def store_line(which, parts, sums):
        gathered[which, line] = joined(dot(basis_t[...], parts)).astype(BF16)
        line_sums[which, line] = tile_of(sums)

    def send_line(which):
        line_gather(gathered.at[which], gather_sem.at[which])
        line_gather(line_sums.at[which], line_sem.at[which])

    def precondition(which, parts):
        local = joined(dot(inverse_ref[:, :owned], parts))
        wait_line(gathered.at[which], gather_sem.at[which], 1)
        products = dot(
            solver[...].reshape(n_plane * width, n_line * width),
            gathered[which].reshape(n_line * width, columns),
        ).reshape(n_plane, width, columns)
        partial[which, :, :width, :] = products
        wait_line(line_sums.at[which], line_sem.at[which], 1)
        line_total = jnp.sum(line_sums[which], axis=0)
        for member in range(n_plane):
            partial[which, member, width:, :] = line_total
        plane_scatter(partial.at[which], received.at[which], partial_sem.at[which])
        received[which, spot] = partial[which, spot]
        wait_margins(2 * which)
        local += dot(inverse_ref[:, owned:], margins[2 * which].reshape(-1, columns))
        wait_plane(received.at[which], partial_sem.at[which], 1)
        total = jnp.sum(received[which], axis=0)
        applied = local + joined(dot(basis_ref[...], halves(total[:width])))
        return applied, total[width:]

    def apply_operator(which, vector):
        exchange = 2 * which + 1
        make_packs(exchange, vector.astype(BF16))
        send_packs(exchange)
        parts = halves(vector)
        size = block_ref.shape[1]
        own = [
            joined(dot(block_ref[block], parts[block * size : (block + 1) * size]))
            for block in range(block_ref.shape[0])
        ]
        own = own[0] if len(own) == 1 else jnp.concatenate(own, axis=0)
        wait_margins(exchange)
        for face in range(4):
            margin = margins[exchange, face]
            own -= dot(spread[0, face], margin) + dot(spread[1, face], margin)
        return own

    operands["coarse"].wait()
    operands["map"].wait()
    repeat(0, coarse_ref.shape[1] // LANES, turn)
    repeat(0, n_plane, arrange)
    operands["rhs"].wait()
    operands["basis"].wait()
    right_side = rhs_ref[...]
    basis_ref[...] = basis_t[...].astype(F32).T.astype(BF16)
    parts = halves(right_side)
    store_line(0, parts, [column_sum(right_side * right_side)])
    operands["rows"].wait()
    operands["weight"].wait()
    row_ids = lax.broadcasted_iota(jnp.int32, (owned, rows_ref.shape[1]), 0)
    for face in range(4):
        hit = row_ids == rows_ref[face : face + 1, :]
        select[face] = jnp.where(hit, 1.0, 0.0).astype(F32).T.astype(BF16)
        weights = jnp.where(hit, weight_ref[face : face + 1, :], 0.0)
        high = weights.astype(BF16)
        spread[0, face] = high
        spread[1, face] = (weights - high.astype(F32)).astype(BF16)
    make_packs(0, right_side.astype(BF16))

    pl.semaphore_wait(barrier, peers)
    plane_scatter(pieces, solver, pieces_sem)
    send_line(0)
    send_packs(0)
    solver[spot] = pieces[spot]
    operands["inverse"].wait()
    operands["block"].wait()
    wait_plane(solver, pieces_sem, 1)

    applied, sums = precondition(0, parts)
    rhs_square = sums[0:1]
    beta = jnp.sqrt(rhs_square + EPSILON)
    one_one = rhs_square / (rhs_square + EPSILON)
    krylov_one = right_side / beta
    precond_one = applied / beta

    image = apply_operator(0, precond_one)
    parts = halves(image)
    store_line(1, parts, [column_sum(image * krylov_one), column_sum(image * image)])
    send_line(1)
    make_packs(2, image.astype(BF16))
    send_packs(2)
    applied, sums = precondition(1, parts)
    first_dot, image_square = sums[0:1], sums[1:2]
    remainder_square = image_square + first_dot * first_dot * (one_one - 2.0)
    remainder_square = jnp.maximum(remainder_square, 0.0)
    first_norm = jnp.sqrt(remainder_square + EPSILON)
    precond_two = (applied - first_dot * precond_one) / first_norm

    krylov_two = (image - first_dot * krylov_one) / first_norm
    one_two = first_dot * (1.0 - one_one) / first_norm
    two_two = remainder_square / (remainder_square + EPSILON)
    image = apply_operator(1, precond_two)
    line_sums[2, line] = tile_of(
        [
            column_sum(image * krylov_one),
            column_sum(image * krylov_two),
            column_sum(image * image),
        ]
    )
    line_gather(line_sums.at[2], line_sem.at[2])
    wait_line(line_sums.at[2], line_sem.at[2], 1)
    plane_sums[spot] = jnp.sum(line_sums[2], axis=0)
    plane_gather(plane_sums, plane_sem)
    wait_plane(plane_sums, plane_sem, 1)
    sums = jnp.sum(plane_sums[...], axis=0)
    cross_dot, second_dot, image_square = sums[0:1], sums[1:2], sums[2:3]
    remainder_square = (
        image_square
        + cross_dot * cross_dot * (one_one - 2.0)
        + second_dot * second_dot * (two_two - 2.0)
        + 2.0 * cross_dot * second_dot * one_two
    )
    second_norm = jnp.sqrt(jnp.maximum(remainder_square, 0.0) + EPSILON)
    weight_one, weight_two, relative = least_squares(
        beta, first_dot, first_norm, cross_dot, second_dot, second_norm
    )
    out_ref[...] = weight_one * precond_one + weight_two * precond_two
    relative_ref[...] = relative

    for which in range(3):
        wait_line(line_sums.at[which], line_sem.at[which], 0)
    wait_plane(plane_sums, plane_sem, 0)
    wait_plane(solver, pieces_sem, 0)
    for which in range(2):
        wait_line(gathered.at[which], gather_sem.at[which], 0)
        wait_plane(received.at[which], partial_sem.at[which], 0)
    for exchange in range(4):
        for face, (_, present, _) in enumerate(faces):

            @pl.when(present)
            def _():
                wait_bytes(packs.at[exchange, face], margin_send.at[exchange, face])


def on_device(
    n_gx,
    n_gy,
    rhs,
    face_rows,
    margin_weight,
    local_blocks,
    subdomain_inverse,
    coarse_basis,
    coarse_inverse,
    coarse_map,
):
    plane = 4 if n_gx % 4 == 0 else 1
    n_line, n_plane = n_gx // plane, plane * n_gy
    owned, columns = rhs.shape[2:]
    margin_rows = face_rows.shape[3]
    width = coarse_basis.shape[3]
    n_coarse = coarse_inverse.shape[3]
    vmem = pl.BlockSpec(memory_space=pltpu.VMEM)
    operands = (
        rhs[0, 0],
        face_rows[0, 0],
        margin_weight[0, 0],
        local_blocks[0, 0],
        subdomain_inverse[0, 0],
        coarse_basis[0, 0].T,
        coarse_inverse[0, 0],
        coarse_map,
    )
    dma = pltpu.SemaphoreType.DMA
    result, relative = pl.pallas_call(
        functools.partial(kernel, n_gx, n_gy, plane),
        out_shape=(
            jax.ShapeDtypeStruct((owned, columns), F32),
            jax.ShapeDtypeStruct((1, columns), F32),
        ),
        in_specs=[pl.BlockSpec(memory_space=pl.ANY)] * len(operands),
        out_specs=(vmem, vmem),
        scratch_shapes=[pltpu.VMEM(each.shape, each.dtype) for each in operands[:-1]]
        + [
            pltpu.SMEM(coarse_map.shape, coarse_map.dtype),
            pltpu.VMEM((n_coarse // width, width, width), F32),
            pltpu.VMEM((n_plane, width, n_line * width), BF16),
            pltpu.VMEM((n_plane, width, n_line * width), BF16),
            pltpu.VMEM((4, margin_rows, owned), BF16),
            pltpu.VMEM((2, 4, owned, margin_rows), BF16),
            pltpu.VMEM((owned, width), BF16),
            pltpu.VMEM((4, 4, margin_rows, columns), BF16),
            pltpu.VMEM((4, 4, margin_rows, columns), BF16),
            pltpu.VMEM((2, n_line, width, columns), BF16),
            pltpu.VMEM((2, n_plane, width + 8, columns), F32),
            pltpu.VMEM((2, n_plane, width + 8, columns), F32),
            pltpu.VMEM((3, n_line, 8, columns), F32),
            pltpu.VMEM((n_plane, 8, columns), F32),
            dma((len(operands),)),
            dma((2,)),
            dma((4, 4)),
            dma((4, 4)),
            dma((2, 2)),
            dma((2, 2)),
            dma((3, 2)),
            dma((2,)),
        ],
        compiler_params=pltpu.CompilerParams(
            collective_id=0, has_side_effects=True, vmem_limit_bytes=56 * 1024 * 1024
        ),
    )(*operands)
    return (result[None, None], relative[0])


def solution(mesh):
    return jax.shard_map(
        functools.partial(on_device, mesh.shape["gx"], mesh.shape["gy"]),
        mesh=mesh,
        in_specs=(
            P("gx", "gy", None, None),
            P("gx", "gy", None, None),
            P("gx", "gy", None, None),
            P("gx", "gy", None, None, None),
            P("gx", "gy", None, None),
            P("gx", "gy", None, None),
            P("gx", "gy", None, None),
            P(),
        ),
        out_specs=(P("gx", "gy", None, None), P()),
        check_vma=False,
    )
```

```python
import functools

import jax
import jax.numpy as jnp
from jax import lax
from jax.experimental import pallas as pl
from jax.experimental.pallas import tpu as pltpu
from jax.sharding import PartitionSpec as P

EPSILON = 1e-06
MESH = pl.DeviceIdType.MESH
F32 = jnp.float32
BF16 = jnp.bfloat16
LANES = 128


def least_squares(scale_norm, first_dot, first_norm, cross_dot, second_dot, second_norm):
    radius_one = jnp.sqrt(first_dot * first_dot + first_norm * first_norm)
    cosine_one = first_dot / radius_one
    sine_one = first_norm / radius_one
    upper_entry = cosine_one * cross_dot + sine_one * second_dot
    lower_entry = cosine_one * second_dot - sine_one * cross_dot
    radius_two = jnp.sqrt(lower_entry * lower_entry + second_norm * second_norm)
    cosine_two = lower_entry / radius_two
    sine_two = second_norm / radius_two
    weight_two = -cosine_two * sine_one * scale_norm / radius_two
    weight_one = (cosine_one * scale_norm - upper_entry * weight_two) / radius_one
    return (weight_one, weight_two, sine_one * sine_two)


def dot(left, right):
    return jnp.dot(left, right, preferred_element_type=F32)


def repeat(first, last, body):
    if last - first <= 8:
        for index in range(first, last):
            body(index)
    else:
        lax.fori_loop(first, last, lambda index, carry: (body(index), carry)[1], 0)


def column_sum(values):
    return jnp.sum(values, axis=0, keepdims=True)


def halves(values):
    high = values.astype(BF16)
    low = (values - high.astype(F32)).astype(BF16)
    return jnp.concatenate([high, low], axis=1)


def joined(values):
    columns = values.shape[1] // 2
    return values[:, :columns] + values[:, columns:]


def kernel(
    n_gx,
    n_gy,
    plane,
    rhs_hbm,
    rows_hbm,
    weight_hbm,
    block_hbm,
    inverse_hbm,
    basis_t_hbm,
    coarse_hbm,
    map_hbm,
    one_hbm,
    two_hbm,
    weights_ref,
    rhs_ref,
    rows_ref,
    weight_ref,
    block_ref,
    inverse_ref,
    basis_t,
    coarse_ref,
    map_ref,
    coarse_t,
    pieces,
    solver,
    select,
    spread,
    basis_ref,
    packs,
    margins,
    gathered,
    partial,
    received,
    line_sums,
    plane_sums,
    results,
    operand_sem,
    result_sem,
    pieces_sem,
    margin_send,
    margin_recv,
    gather_sem,
    partial_sem,
    line_sem,
    plane_sem,
):
    i = lax.axis_index("gx")
    j = lax.axis_index("gy")
    n_line = n_gx // plane
    n_plane = plane * n_gy
    line = i // plane
    spot = (i % plane) * n_gy + j
    owned, columns = rhs_ref.shape
    width = basis_ref.shape[1]

    def line_device(slot):
        return (slot * plane + i % plane, j)

    def plane_device(slot):
        return (line * plane + slot // n_gy, slot % n_gy)

    barrier = pltpu.get_barrier_semaphore()

    def greet(device):
        pl.semaphore_signal(barrier, inc=1, device_id=device, device_id_type=MESH)

    repeat(1, n_line, lambda step: greet(line_device((line + step) % n_line)))
    repeat(1, n_plane, lambda step: greet(plane_device((spot + step) % n_plane)))
    cross_down = jnp.logical_and(i % plane == 0, i > 0)
    cross_up = jnp.logical_and(i % plane == plane - 1, i < n_gx - 1)
    peers = n_line + n_plane - 2
    if plane > 1:
        peers += cross_down.astype(jnp.int32) + cross_up.astype(jnp.int32)

        @pl.when(cross_down)
        def _():
            greet((i - 1, j))

        @pl.when(cross_up)
        def _():
            greet((i + 1, j))

    operands = {}
    for index, (name, source, target) in enumerate(
        (
            ("coarse", coarse_hbm, coarse_ref),
            ("map", map_hbm, map_ref),
            ("rhs", rhs_hbm, rhs_ref),
            ("basis", basis_t_hbm, basis_t),
            ("rows", rows_hbm, rows_ref),
            ("weight", weight_hbm, weight_ref),
            ("inverse", inverse_hbm, inverse_ref),
            ("block", block_hbm, block_ref),
        )
    ):
        operands[name] = pltpu.make_async_copy(source, target, operand_sem.at[index])
        operands[name].start()

    faces = (
        ((i - 1, j), i > 0, 1),
        ((i + 1, j), i < n_gx - 1, 0),
        ((i, j - 1), j > 0, 3),
        ((i, j + 1), j < n_gy - 1, 2),
    )

    for face, (_, present, _) in enumerate(faces):

        @pl.when(jnp.logical_not(present))
        def _():
            for exchange in range(margins.shape[0]):
                margins[exchange, face] = jnp.zeros(margins.shape[2:], BF16)

    def start_copy(source, target, sends, recvs, device):
        pltpu.make_async_remote_copy(
            src_ref=source,
            dst_ref=target,
            send_sem=sends,
            recv_sem=recvs,
            device_id=device,
            device_id_type=MESH,
        ).start()

    def wait_bytes(ref, sem):
        pltpu.make_async_copy(ref, ref, sem).wait()

    def line_gather(slots, sems):
        def send(step):
            device = line_device((line + step) % n_line)
            start_copy(slots.at[line], slots.at[line], sems.at[0], sems.at[1], device)

        repeat(1, n_line, send)

    def plane_gather(slots, sems):
        def send(step):
            device = plane_device((spot + step) % n_plane)
            start_copy(slots.at[spot], slots.at[spot], sems.at[0], sems.at[1], device)

        repeat(1, n_plane, send)

    def plane_scatter(sources, slots, sems):
        def send(step):
            other = (spot + step) % n_plane
            start_copy(
                sources.at[other], slots.at[spot], sems.at[0], sems.at[1], plane_device(other)
            )

        repeat(1, n_plane, send)

    def wait_line(slots, sems, which):
        if n_line > 1:
            wait_bytes(slots.at[pl.ds(0, n_line - 1)], sems.at[which])

    def wait_plane(slots, sems, which):
        if n_plane > 1:
            wait_bytes(slots.at[pl.ds(0, n_plane - 1)], sems.at[which])

    def tile_of(sums):
        rest = jnp.zeros((8 - len(sums), columns), F32)
        return jnp.concatenate(list(sums) + [rest], axis=0)

    def turn(chunk):
        start = chunk * LANES
        if not isinstance(start, int):
            start = pl.multiple_of(start, LANES)
        turned = coarse_ref[:, pl.ds(start, LANES)].astype(F32).T
        count = LANES // width
        coarse_t[pl.ds(chunk * count, count)] = turned.reshape(count, width, width)

    def arrange(member):
        parts = []
        for other_line in range(n_line):
            parts.append(coarse_t[map_ref[other_line * n_plane + member]])
        pieces[member] = jnp.concatenate(parts, axis=0).T.astype(BF16)

    def make_packs(exchange, rounded):
        packs[exchange] = (
            dot(select[...].reshape(-1, owned), rounded)
            .astype(BF16)
            .reshape(packs.shape[1:])
        )

    def send_packs(exchange):
        for face, (device, present, block) in enumerate(faces):

            @pl.when(present)
            def _():
                start_copy(
                    packs.at[exchange, face],
                    margins.at[exchange, block],
                    margin_send.at[exchange, face],
                    margin_recv.at[exchange, block],
                    device,
                )

    def wait_margins(exchange):
        for face, (_, present, _) in enumerate(faces):

            @pl.when(present)
            def _():
                wait_bytes(margins.at[exchange, face], margin_recv.at[exchange, face])

    def store_line(which, parts, sums):
        gathered[which, line] = joined(dot(basis_t[...], parts)).astype(BF16)
        line_sums[which, line] = tile_of(sums)

    def send_line(which):
        line_gather(gathered.at[which], gather_sem.at[which])
        line_gather(line_sums.at[which], line_sem.at[which])

    def precondition(which, parts):
        local = joined(dot(inverse_ref[:, :owned], parts))
        wait_line(gathered.at[which], gather_sem.at[which], 1)
        products = dot(
            solver[...].reshape(n_plane * width, n_line * width),
            gathered[which].reshape(n_line * width, columns),
        ).reshape(n_plane, width, columns)
        partial[which, :, :width, :] = products
        wait_line(line_sums.at[which], line_sem.at[which], 1)
        line_total = jnp.sum(line_sums[which], axis=0)
        for member in range(n_plane):
            partial[which, member, width:, :] = line_total
        plane_scatter(partial.at[which], received.at[which], partial_sem.at[which])
        received[which, spot] = partial[which, spot]
        wait_margins(2 * which)
        local += dot(inverse_ref[:, owned:], margins[2 * which].reshape(-1, columns))
        wait_plane(received.at[which], partial_sem.at[which], 1)
        total = jnp.sum(received[which], axis=0)
        applied = local + joined(dot(basis_ref[...], halves(total[:width])))
        return applied, total[width:]

    def apply_operator(which, vector):
        exchange = 2 * which + 1
        make_packs(exchange, vector.astype(BF16))
        send_packs(exchange)
        parts = halves(vector)
        size = block_ref.shape[1]
        own = [
            joined(dot(block_ref[block], parts[block * size : (block + 1) * size]))
            for block in range(block_ref.shape[0])
        ]
        own = own[0] if len(own) == 1 else jnp.concatenate(own, axis=0)
        wait_margins(exchange)
        for face in range(4):
            margin = margins[exchange, face]
            own -= dot(spread[0, face], margin) + dot(spread[1, face], margin)
        return own

    operands["coarse"].wait()
    operands["map"].wait()
    repeat(0, coarse_ref.shape[1] // LANES, turn)
    repeat(0, n_plane, arrange)
    operands["rhs"].wait()
    operands["basis"].wait()
    right_side = rhs_ref[...]
    basis_ref[...] = basis_t[...].astype(F32).T.astype(BF16)
    parts = halves(right_side)
    store_line(0, parts, [column_sum(right_side * right_side)])
    operands["rows"].wait()
    operands["weight"].wait()
    row_ids = lax.broadcasted_iota(jnp.int32, (owned, rows_ref.shape[1]), 0)
    for face in range(4):
        hit = row_ids == rows_ref[face : face + 1, :]
        select[face] = jnp.where(hit, 1.0, 0.0).astype(F32).T.astype(BF16)
        weights = jnp.where(hit, weight_ref[face : face + 1, :], 0.0)
        high = weights.astype(BF16)
        spread[0, face] = high
        spread[1, face] = (weights - high.astype(F32)).astype(BF16)
    make_packs(0, right_side.astype(BF16))

    pl.semaphore_wait(barrier, peers)
    plane_scatter(pieces, solver, pieces_sem)
    send_line(0)
    send_packs(0)
    solver[spot] = pieces[spot]
    operands["inverse"].wait()
    operands["block"].wait()
    wait_plane(solver, pieces_sem, 1)

    applied, sums = precondition(0, parts)
    rhs_square = sums[0:1]
    beta = jnp.sqrt(rhs_square + EPSILON)
    one_one = rhs_square / (rhs_square + EPSILON)
    krylov_one = right_side / beta
    precond_one = applied / beta
    results[0] = precond_one
    first_result = pltpu.make_async_copy(results.at[0], one_hbm, result_sem.at[0])
    first_result.start()

    image = apply_operator(0, precond_one)
    parts = halves(image)
    store_line(1, parts, [column_sum(image * krylov_one), column_sum(image * image)])
    send_line(1)
    make_packs(2, image.astype(BF16))
    send_packs(2)
    applied, sums = precondition(1, parts)
    first_dot, image_square = sums[0:1], sums[1:2]
    remainder_square = image_square + first_dot * first_dot * (one_one - 2.0)
    remainder_square = jnp.maximum(remainder_square, 0.0)
    first_norm = jnp.sqrt(remainder_square + EPSILON)
    precond_two = (applied - first_dot * precond_one) / first_norm
    results[1] = precond_two
    second_result = pltpu.make_async_copy(results.at[1], two_hbm, result_sem.at[1])
    second_result.start()

    krylov_two = (image - first_dot * krylov_one) / first_norm
    one_two = first_dot * (1.0 - one_one) / first_norm
    two_two = remainder_square / (remainder_square + EPSILON)
    image = apply_operator(1, precond_two)
    line_sums[2, line] = tile_of(
        [
            column_sum(image * krylov_one),
            column_sum(image * krylov_two),
            column_sum(image * image),
        ]
    )
    line_gather(line_sums.at[2], line_sem.at[2])
    wait_line(line_sums.at[2], line_sem.at[2], 1)
    plane_sums[spot] = jnp.sum(line_sums[2], axis=0)
    plane_gather(plane_sums, plane_sem)
    wait_plane(plane_sums, plane_sem, 1)
    sums = jnp.sum(plane_sums[...], axis=0)
    cross_dot, second_dot, image_square = sums[0:1], sums[1:2], sums[2:3]
    remainder_square = (
        image_square
        + cross_dot * cross_dot * (one_one - 2.0)
        + second_dot * second_dot * (two_two - 2.0)
        + 2.0 * cross_dot * second_dot * one_two
    )
    second_norm = jnp.sqrt(jnp.maximum(remainder_square, 0.0) + EPSILON)
    weight_one, weight_two, relative = least_squares(
        beta, first_dot, first_norm, cross_dot, second_dot, second_norm
    )
    weights_ref[...] = tile_of([weight_one, weight_two, relative])
    first_result.wait()
    second_result.wait()

    for which in range(3):
        wait_line(line_sums.at[which], line_sem.at[which], 0)
    wait_plane(plane_sums, plane_sem, 0)
    wait_plane(solver, pieces_sem, 0)
    for which in range(2):
        wait_line(gathered.at[which], gather_sem.at[which], 0)
        wait_plane(received.at[which], partial_sem.at[which], 0)
    for exchange in range(4):
        for face, (_, present, _) in enumerate(faces):

            @pl.when(present)
            def _():
                wait_bytes(packs.at[exchange, face], margin_send.at[exchange, face])


def on_device(
    n_gx,
    n_gy,
    rhs,
    face_rows,
    margin_weight,
    local_blocks,
    subdomain_inverse,
    coarse_basis,
    coarse_inverse,
    coarse_map,
):
    plane = 4 if n_gx % 4 == 0 else 1
    n_line, n_plane = n_gx // plane, plane * n_gy
    owned, columns = rhs.shape[2:]
    margin_rows = face_rows.shape[3]
    width = coarse_basis.shape[3]
    n_coarse = coarse_inverse.shape[3]
    vmem = pl.BlockSpec(memory_space=pltpu.VMEM)
    hbm = pl.BlockSpec(memory_space=pl.ANY)
    operands = (
        rhs[0, 0],
        face_rows[0, 0],
        margin_weight[0, 0],
        local_blocks[0, 0],
        subdomain_inverse[0, 0],
        coarse_basis[0, 0].T,
        coarse_inverse[0, 0],
        coarse_map,
    )
    dma = pltpu.SemaphoreType.DMA
    one, two, weights = pl.pallas_call(
        functools.partial(kernel, n_gx, n_gy, plane),
        out_shape=(
            jax.ShapeDtypeStruct((owned, columns), F32),
            jax.ShapeDtypeStruct((owned, columns), F32),
            jax.ShapeDtypeStruct((8, columns), F32),
        ),
        in_specs=[hbm] * len(operands),
        out_specs=(hbm, hbm, vmem),
        scratch_shapes=[pltpu.VMEM(each.shape, each.dtype) for each in operands[:-1]]
        + [
            pltpu.SMEM(coarse_map.shape, coarse_map.dtype),
            pltpu.VMEM((n_coarse // width, width, width), F32),
            pltpu.VMEM((n_plane, width, n_line * width), BF16),
            pltpu.VMEM((n_plane, width, n_line * width), BF16),
            pltpu.VMEM((4, margin_rows, owned), BF16),
            pltpu.VMEM((2, 4, owned, margin_rows), BF16),
            pltpu.VMEM((owned, width), BF16),
            pltpu.VMEM((4, 4, margin_rows, columns), BF16),
            pltpu.VMEM((4, 4, margin_rows, columns), BF16),
            pltpu.VMEM((2, n_line, width, columns), BF16),
            pltpu.VMEM((2, n_plane, width + 8, columns), F32),
            pltpu.VMEM((2, n_plane, width + 8, columns), F32),
            pltpu.VMEM((3, n_line, 8, columns), F32),
            pltpu.VMEM((n_plane, 8, columns), F32),
            pltpu.VMEM((2, owned, columns), F32),
            dma((len(operands),)),
            dma((2,)),
            dma((2,)),
            dma((4, 4)),
            dma((4, 4)),
            dma((2, 2)),
            dma((2, 2)),
            dma((3, 2)),
            dma((2,)),
        ],
        compiler_params=pltpu.CompilerParams(
            collective_id=0, has_side_effects=True, vmem_limit_bytes=56 * 1024 * 1024
        ),
    )(*operands)
    result = weights[0:1] * one + weights[1:2] * two
    return (result[None, None], weights[2])


def solution(mesh):
    return jax.shard_map(
        functools.partial(on_device, mesh.shape["gx"], mesh.shape["gy"]),
        mesh=mesh,
        in_specs=(
            P("gx", "gy", None, None),
            P("gx", "gy", None, None),
            P("gx", "gy", None, None),
            P("gx", "gy", None, None, None),
            P("gx", "gy", None, None),
            P("gx", "gy", None, None),
            P("gx", "gy", None, None),
            P(),
        ),
        out_specs=(P("gx", "gy", None, None), P()),
        check_vma=False,
    )
```

```python
import functools

import jax
import jax.numpy as jnp
from jax import lax
from jax.experimental import pallas as pl
from jax.experimental.pallas import tpu as pltpu
from jax.sharding import PartitionSpec as P

EPSILON = 1e-06
MESH = pl.DeviceIdType.MESH
F32 = jnp.float32
BF16 = jnp.bfloat16
LANES = 128


def least_squares(scale_norm, first_dot, first_norm, cross_dot, second_dot, second_norm):
    radius_one = jnp.sqrt(first_dot * first_dot + first_norm * first_norm)
    cosine_one = first_dot / radius_one
    sine_one = first_norm / radius_one
    upper_entry = cosine_one * cross_dot + sine_one * second_dot
    lower_entry = cosine_one * second_dot - sine_one * cross_dot
    radius_two = jnp.sqrt(lower_entry * lower_entry + second_norm * second_norm)
    cosine_two = lower_entry / radius_two
    sine_two = second_norm / radius_two
    weight_two = -cosine_two * sine_one * scale_norm / radius_two
    weight_one = (cosine_one * scale_norm - upper_entry * weight_two) / radius_one
    return (weight_one, weight_two, sine_one * sine_two)


def dot(left, right):
    return jnp.dot(left, right, preferred_element_type=F32)


def repeat(first, last, body):
    if last - first <= 8:
        for index in range(first, last):
            body(index)
    else:
        lax.fori_loop(first, last, lambda index, carry: (body(index), carry)[1], 0)


def column_sum(values):
    return jnp.sum(values, axis=0, keepdims=True)


def halves(values):
    high = values.astype(BF16)
    low = (values - high.astype(F32)).astype(BF16)
    return jnp.concatenate([high, low], axis=1)


def joined(values):
    columns = values.shape[1] // 2
    return values[:, :columns] + values[:, columns:]


def kernel(
    n_gx,
    n_gy,
    plane,
    rhs_hbm,
    rows_hbm,
    weight_hbm,
    block_hbm,
    inverse_hbm,
    basis_t_hbm,
    coarse_hbm,
    map_hbm,
    out_ref,
    relative_ref,
    rhs_ref,
    rows_ref,
    weight_ref,
    block_ref,
    inverse_ref,
    basis_t,
    coarse_ref,
    map_ref,
    coarse_t,
    pieces,
    solver,
    select,
    spread,
    basis_ref,
    packs,
    margins,
    gathered,
    partial,
    received,
    line_sums,
    plane_sums,
    basis_packs,
    basis_margins,
    fold,
    solved,
    solved_margins,
    operand_sem,
    basis_send,
    basis_recv,
    solved_send,
    solved_recv,
    pieces_sem,
    margin_send,
    margin_recv,
    gather_sem,
    partial_sem,
    line_sem,
    plane_sem,
):
    i = lax.axis_index("gx")
    j = lax.axis_index("gy")
    n_line = n_gx // plane
    n_plane = plane * n_gy
    line = i // plane
    spot = (i % plane) * n_gy + j
    owned, columns = rhs_ref.shape
    width = basis_ref.shape[1]

    def line_device(slot):
        return (slot * plane + i % plane, j)

    def plane_device(slot):
        return (line * plane + slot // n_gy, slot % n_gy)

    barrier = pltpu.get_barrier_semaphore()

    def greet(device):
        pl.semaphore_signal(barrier, inc=1, device_id=device, device_id_type=MESH)

    repeat(1, n_line, lambda step: greet(line_device((line + step) % n_line)))
    repeat(1, n_plane, lambda step: greet(plane_device((spot + step) % n_plane)))
    cross_down = jnp.logical_and(i % plane == 0, i > 0)
    cross_up = jnp.logical_and(i % plane == plane - 1, i < n_gx - 1)
    peers = n_line + n_plane - 2
    if plane > 1:
        peers += cross_down.astype(jnp.int32) + cross_up.astype(jnp.int32)

        @pl.when(cross_down)
        def _():
            greet((i - 1, j))

        @pl.when(cross_up)
        def _():
            greet((i + 1, j))

    operands = {}
    for index, (name, source, target) in enumerate(
        (
            ("coarse", coarse_hbm, coarse_ref),
            ("map", map_hbm, map_ref),
            ("rhs", rhs_hbm, rhs_ref),
            ("basis", basis_t_hbm, basis_t),
            ("rows", rows_hbm, rows_ref),
            ("weight", weight_hbm, weight_ref),
            ("inverse", inverse_hbm, inverse_ref),
            ("block", block_hbm, block_ref),
        )
    ):
        operands[name] = pltpu.make_async_copy(source, target, operand_sem.at[index])
        operands[name].start()

    faces = (
        ((i - 1, j), i > 0, 1),
        ((i + 1, j), i < n_gx - 1, 0),
        ((i, j - 1), j > 0, 3),
        ((i, j + 1), j < n_gy - 1, 2),
    )

    for face, (_, present, _) in enumerate(faces):

        @pl.when(jnp.logical_not(present))
        def _():
            for exchange in range(margins.shape[0]):
                margins[exchange, face] = jnp.zeros(margins.shape[2:], BF16)
            for which in range(solved_margins.shape[0]):
                solved_margins[which, face] = jnp.zeros(solved_margins.shape[2:], BF16)
            basis_margins[face] = jnp.zeros(basis_margins.shape[1:], BF16)

    def start_copy(source, target, sends, recvs, device):
        pltpu.make_async_remote_copy(
            src_ref=source,
            dst_ref=target,
            send_sem=sends,
            recv_sem=recvs,
            device_id=device,
            device_id_type=MESH,
        ).start()

    def wait_bytes(ref, sem):
        pltpu.make_async_copy(ref, ref, sem).wait()

    def line_gather(slots, sems):
        def send(step):
            device = line_device((line + step) % n_line)
            start_copy(slots.at[line], slots.at[line], sems.at[0], sems.at[1], device)

        repeat(1, n_line, send)

    def plane_gather(slots, sems):
        def send(step):
            device = plane_device((spot + step) % n_plane)
            start_copy(slots.at[spot], slots.at[spot], sems.at[0], sems.at[1], device)

        repeat(1, n_plane, send)

    def plane_scatter(sources, slots, sems):
        def send(step):
            other = (spot + step) % n_plane
            start_copy(
                sources.at[other], slots.at[spot], sems.at[0], sems.at[1], plane_device(other)
            )

        repeat(1, n_plane, send)

    def wait_line(slots, sems, which):
        if n_line > 1:
            wait_bytes(slots.at[pl.ds(0, n_line - 1)], sems.at[which])

    def wait_plane(slots, sems, which):
        if n_plane > 1:
            wait_bytes(slots.at[pl.ds(0, n_plane - 1)], sems.at[which])

    def tile_of(sums):
        rest = jnp.zeros((8 - len(sums), columns), F32)
        return jnp.concatenate(list(sums) + [rest], axis=0)

    def turn(chunk):
        start = chunk * LANES
        if not isinstance(start, int):
            start = pl.multiple_of(start, LANES)
        turned = coarse_ref[:, pl.ds(start, LANES)].astype(F32).T
        count = LANES // width
        coarse_t[pl.ds(chunk * count, count)] = turned.reshape(count, width, width)

    def arrange(member):
        parts = []
        for other_line in range(n_line):
            parts.append(coarse_t[map_ref[other_line * n_plane + member]])
        pieces[member] = jnp.concatenate(parts, axis=0).T.astype(BF16)

    def make_packs(exchange, rounded):
        packs[exchange] = (
            dot(select[...].reshape(-1, owned), rounded)
            .astype(BF16)
            .reshape(packs.shape[1:])
        )

    def send_faces(sources, targets, sends, recvs):
        for face, (device, present, block) in enumerate(faces):

            @pl.when(present)
            def _():
                start_copy(
                    sources[face], targets.at[block], sends.at[face], recvs.at[block], device
                )

    def wait_faces(targets, sems):
        for face, (_, present, _) in enumerate(faces):

            @pl.when(present)
            def _():
                wait_bytes(targets.at[face], sems.at[face])

    def send_packs(exchange):
        send_faces(
            [packs.at[exchange, face] for face in range(4)],
            margins.at[exchange],
            margin_send.at[exchange],
            margin_recv.at[exchange],
        )

    def wait_margins(exchange):
        wait_faces(margins.at[exchange], margin_recv.at[exchange])

    def store_line(which, parts, sums):
        gathered[which, line] = joined(dot(basis_t[...], parts)).astype(BF16)
        line_sums[which, line] = tile_of(sums)

    def send_line(which):
        line_gather(gathered.at[which], gather_sem.at[which])
        line_gather(line_sums.at[which], line_sem.at[which])

    def fold_basis():
        wait_faces(basis_margins, basis_recv)
        folds = []
        for face in range(4):
            folds.append(
                sum(
                    lax.dot_general(
                        spread[part, face],
                        basis_margins[face],
                        (((1,), (1,)), ((), ())),
                        preferred_element_type=F32,
                    )
                    for part in range(2)
                )
            )
        fold[...] = halves(jnp.concatenate(folds, axis=1))

    def apply_both(which, parts):
        local = joined(dot(inverse_ref[:, :owned], parts))
        wait_line(gathered.at[which], gather_sem.at[which], 1)
        products = dot(
            solver[...].reshape(n_plane * width, n_line * width),
            gathered[which].reshape(n_line * width, columns),
        ).reshape(n_plane, width, columns)
        partial[which, :, :width, :] = products
        wait_line(line_sums.at[which], line_sem.at[which], 1)
        line_total = jnp.sum(line_sums[which], axis=0)
        for member in range(n_plane):
            partial[which, member, width:, :] = line_total
        plane_scatter(partial.at[which], received.at[which], partial_sem.at[which])
        received[which, spot] = partial[which, spot]
        wait_margins(2 * which)
        local += dot(inverse_ref[:, owned:], margins[2 * which].reshape(-1, columns))
        make_packs(2 * which + 1, local.astype(BF16))
        send_packs(2 * which + 1)
        if which == 0:
            fold_basis()
        wait_plane(received.at[which], partial_sem.at[which], 1)
        total = jnp.sum(received[which], axis=0)
        solved[which] = total[:width].astype(BF16)
        send_faces(
            [solved.at[which]] * 4,
            solved_margins.at[which],
            solved_send.at[which],
            solved_recv.at[which],
        )
        applied = local + joined(dot(basis_ref[...], halves(total[:width])))
        halved = halves(applied)
        size = block_ref.shape[1]
        own = [
            joined(dot(block_ref[block], halved[block * size : (block + 1) * size]))
            for block in range(block_ref.shape[0])
        ]
        own = own[0] if len(own) == 1 else jnp.concatenate(own, axis=0)
        wait_margins(2 * which + 1)
        for face in range(4):
            margin = margins[2 * which + 1, face]
            own -= dot(spread[0, face], margin) + dot(spread[1, face], margin)
        wait_faces(solved_margins.at[which], solved_recv.at[which])
        coarse = solved_margins[which].reshape(4 * width, columns)
        own -= dot(fold[...], jnp.concatenate([coarse, coarse], axis=0))
        return applied, own, total[width:]

    operands["coarse"].wait()
    operands["map"].wait()
    repeat(0, coarse_ref.shape[1] // LANES, turn)
    repeat(0, n_plane, arrange)
    operands["rhs"].wait()
    operands["basis"].wait()
    right_side = rhs_ref[...]
    basis_ref[...] = basis_t[...].astype(F32).T.astype(BF16)
    parts = halves(right_side)
    store_line(0, parts, [column_sum(right_side * right_side)])
    operands["rows"].wait()
    operands["weight"].wait()
    row_ids = lax.broadcasted_iota(jnp.int32, (owned, rows_ref.shape[1]), 0)
    for face in range(4):
        hit = row_ids == rows_ref[face : face + 1, :]
        one_hot = jnp.where(hit, 1.0, 0.0).astype(F32)
        select[face] = one_hot.T.astype(BF16)
        basis_packs[face] = dot(basis_t[...], one_hot.astype(BF16)).astype(BF16)
        weights = jnp.where(hit, weight_ref[face : face + 1, :], 0.0)
        high = weights.astype(BF16)
        spread[0, face] = high
        spread[1, face] = (weights - high.astype(F32)).astype(BF16)
    make_packs(0, right_side.astype(BF16))

    pl.semaphore_wait(barrier, peers)
    plane_scatter(pieces, solver, pieces_sem)
    send_line(0)
    send_packs(0)
    send_faces(
        [basis_packs.at[face] for face in range(4)], basis_margins, basis_send, basis_recv
    )
    solver[spot] = pieces[spot]
    operands["inverse"].wait()
    operands["block"].wait()
    wait_plane(solver, pieces_sem, 1)

    applied, image, sums = apply_both(0, parts)
    rhs_square = sums[0:1]
    beta = jnp.sqrt(rhs_square + EPSILON)
    one_one = rhs_square / (rhs_square + EPSILON)
    krylov_one = right_side / beta
    image_one = image / beta

    parts = halves(image_one)
    store_line(
        1, parts, [column_sum(image_one * krylov_one), column_sum(image_one * image_one)]
    )
    send_line(1)
    make_packs(2, image_one.astype(BF16))
    send_packs(2)
    precond_one = applied / beta
    applied, image, sums = apply_both(1, parts)
    first_dot, image_square = sums[0:1], sums[1:2]
    remainder_square = image_square + first_dot * first_dot * (one_one - 2.0)
    remainder_square = jnp.maximum(remainder_square, 0.0)
    first_norm = jnp.sqrt(remainder_square + EPSILON)
    precond_two = (applied - first_dot * precond_one) / first_norm

    krylov_two = (image_one - first_dot * krylov_one) / first_norm
    one_two = first_dot * (1.0 - one_one) / first_norm
    two_two = remainder_square / (remainder_square + EPSILON)
    image = (image - first_dot * image_one) / first_norm
    line_sums[2, line] = tile_of(
        [
            column_sum(image * krylov_one),
            column_sum(image * krylov_two),
            column_sum(image * image),
        ]
    )
    line_gather(line_sums.at[2], line_sem.at[2])
    wait_line(line_sums.at[2], line_sem.at[2], 1)
    plane_sums[spot] = jnp.sum(line_sums[2], axis=0)
    plane_gather(plane_sums, plane_sem)
    wait_plane(plane_sums, plane_sem, 1)
    sums = jnp.sum(plane_sums[...], axis=0)
    cross_dot, second_dot, image_square = sums[0:1], sums[1:2], sums[2:3]
    remainder_square = (
        image_square
        + cross_dot * cross_dot * (one_one - 2.0)
        + second_dot * second_dot * (two_two - 2.0)
        + 2.0 * cross_dot * second_dot * one_two
    )
    second_norm = jnp.sqrt(jnp.maximum(remainder_square, 0.0) + EPSILON)
    weight_one, weight_two, relative = least_squares(
        beta, first_dot, first_norm, cross_dot, second_dot, second_norm
    )
    out_ref[...] = weight_one * precond_one + weight_two * precond_two
    relative_ref[...] = relative

    for which in range(3):
        wait_line(line_sums.at[which], line_sem.at[which], 0)
    wait_plane(plane_sums, plane_sem, 0)
    wait_plane(solver, pieces_sem, 0)
    for which in range(2):
        wait_line(gathered.at[which], gather_sem.at[which], 0)
        wait_plane(received.at[which], partial_sem.at[which], 0)
    for exchange in range(4):
        for face, (_, present, _) in enumerate(faces):

            @pl.when(present)
            def _():
                wait_bytes(packs.at[exchange, face], margin_send.at[exchange, face])

    wait_faces(basis_packs, basis_send)
    for which in range(2):
        wait_faces(solved_margins.at[which], solved_send.at[which])


def on_device(
    n_gx,
    n_gy,
    rhs,
    face_rows,
    margin_weight,
    local_blocks,
    subdomain_inverse,
    coarse_basis,
    coarse_inverse,
    coarse_map,
):
    plane = 4 if n_gx % 4 == 0 else 1
    n_line, n_plane = n_gx // plane, plane * n_gy
    owned, columns = rhs.shape[2:]
    margin_rows = face_rows.shape[3]
    width = coarse_basis.shape[3]
    n_coarse = coarse_inverse.shape[3]
    vmem = pl.BlockSpec(memory_space=pltpu.VMEM)
    operands = (
        rhs[0, 0],
        face_rows[0, 0],
        margin_weight[0, 0],
        local_blocks[0, 0],
        subdomain_inverse[0, 0],
        coarse_basis[0, 0].T,
        coarse_inverse[0, 0],
        coarse_map,
    )
    dma = pltpu.SemaphoreType.DMA
    result, relative = pl.pallas_call(
        functools.partial(kernel, n_gx, n_gy, plane),
        out_shape=(
            jax.ShapeDtypeStruct((owned, columns), F32),
            jax.ShapeDtypeStruct((1, columns), F32),
        ),
        in_specs=[pl.BlockSpec(memory_space=pl.ANY)] * len(operands),
        out_specs=(vmem, vmem),
        scratch_shapes=[pltpu.VMEM(each.shape, each.dtype) for each in operands[:-1]]
        + [
            pltpu.SMEM(coarse_map.shape, coarse_map.dtype),
            pltpu.VMEM((n_coarse // width, width, width), F32),
            pltpu.VMEM((n_plane, width, n_line * width), BF16),
            pltpu.VMEM((n_plane, width, n_line * width), BF16),
            pltpu.VMEM((4, margin_rows, owned), BF16),
            pltpu.VMEM((2, 4, owned, margin_rows), BF16),
            pltpu.VMEM((owned, width), BF16),
            pltpu.VMEM((4, 4, margin_rows, columns), BF16),
            pltpu.VMEM((4, 4, margin_rows, columns), BF16),
            pltpu.VMEM((2, n_line, width, columns), BF16),
            pltpu.VMEM((2, n_plane, width + 8, columns), F32),
            pltpu.VMEM((2, n_plane, width + 8, columns), F32),
            pltpu.VMEM((3, n_line, 8, columns), F32),
            pltpu.VMEM((n_plane, 8, columns), F32),
            pltpu.VMEM((4, width, margin_rows), BF16),
            pltpu.VMEM((4, width, margin_rows), BF16),
            pltpu.VMEM((owned, 8 * width), BF16),
            pltpu.VMEM((2, width, columns), BF16),
            pltpu.VMEM((2, 4, width, columns), BF16),
            dma((len(operands),)),
            dma((4,)),
            dma((4,)),
            dma((2, 4)),
            dma((2, 4)),
            dma((2,)),
            dma((4, 4)),
            dma((4, 4)),
            dma((2, 2)),
            dma((2, 2)),
            dma((3, 2)),
            dma((2,)),
        ],
        compiler_params=pltpu.CompilerParams(
            collective_id=0, has_side_effects=True, vmem_limit_bytes=56 * 1024 * 1024
        ),
    )(*operands)
    return (result[None, None], relative[0])


def solution(mesh):
    return jax.shard_map(
        functools.partial(on_device, mesh.shape["gx"], mesh.shape["gy"]),
        mesh=mesh,
        in_specs=(
            P("gx", "gy", None, None),
            P("gx", "gy", None, None),
            P("gx", "gy", None, None),
            P("gx", "gy", None, None, None),
            P("gx", "gy", None, None),
            P("gx", "gy", None, None),
            P("gx", "gy", None, None),
            P(),
        ),
        out_specs=(P("gx", "gy", None, None), P()),
        check_vma=False,
    )
```

```python
import functools

import jax
import jax.numpy as jnp
from jax import lax
from jax.experimental import pallas as pl
from jax.experimental.pallas import tpu as pltpu
from jax.sharding import PartitionSpec as P

EPSILON = 1e-06
MESH = pl.DeviceIdType.MESH
F32 = jnp.float32
BF16 = jnp.bfloat16
LANES = 128


def least_squares(scale_norm, first_dot, first_norm, cross_dot, second_dot, second_norm):
    radius_one = jnp.sqrt(first_dot * first_dot + first_norm * first_norm)
    cosine_one = first_dot / radius_one
    sine_one = first_norm / radius_one
    upper_entry = cosine_one * cross_dot + sine_one * second_dot
    lower_entry = cosine_one * second_dot - sine_one * cross_dot
    radius_two = jnp.sqrt(lower_entry * lower_entry + second_norm * second_norm)
    cosine_two = lower_entry / radius_two
    sine_two = second_norm / radius_two
    weight_two = -cosine_two * sine_one * scale_norm / radius_two
    weight_one = (cosine_one * scale_norm - upper_entry * weight_two) / radius_one
    return (weight_one, weight_two, sine_one * sine_two)


def dot(left, right):
    return jnp.dot(left, right, preferred_element_type=F32)


def repeat(first, last, body, unrolled=8):
    if last - first <= unrolled:
        for index in range(first, last):
            body(index)
    else:
        lax.fori_loop(first, last, lambda index, carry: (body(index), carry)[1], 0)


def column_sum(values):
    return jnp.sum(values, axis=0, keepdims=True)


def halves(values):
    high = values.astype(BF16)
    low = (values - high.astype(F32)).astype(BF16)
    return jnp.concatenate([high, low], axis=1)


def joined(values):
    columns = values.shape[1] // 2
    return values[:, :columns] + values[:, columns:]


def kernel(
    n_gx,
    n_gy,
    plane,
    rhs_hbm,
    rows_hbm,
    weight_hbm,
    block_hbm,
    inverse_hbm,
    basis_t_hbm,
    coarse_hbm,
    map_hbm,
    out_ref,
    relative_ref,
    rhs_ref,
    rows_ref,
    weight_ref,
    block_ref,
    inverse_ref,
    basis_t,
    coarse_ref,
    map_ref,
    coarse_t,
    pieces,
    solver,
    select,
    spread,
    basis_ref,
    packs,
    margins,
    gathered,
    partial,
    received,
    line_sums,
    all_sums,
    basis_packs,
    basis_margins,
    fold,
    solved,
    solved_margins,
    operand_sem,
    basis_send,
    basis_recv,
    solved_send,
    solved_recv,
    pieces_sem,
    margin_send,
    margin_recv,
    gather_sem,
    partial_sem,
    line_sem,
    all_sem,
):
    i = lax.axis_index("gx")
    j = lax.axis_index("gy")
    n_line = n_gx // plane
    n_plane = plane * n_gy
    line = i // plane
    spot = (i % plane) * n_gy + j
    owned, columns = rhs_ref.shape
    width = basis_ref.shape[1]

    def line_device(slot):
        return (slot * plane + i % plane, j)

    def plane_device(slot):
        return (line * plane + slot // n_gy, slot % n_gy)

    barrier = pltpu.get_barrier_semaphore()

    def greet(device):
        pl.semaphore_signal(barrier, inc=1, device_id=device, device_id_type=MESH)

    n_all = n_gx * n_gy
    place = i * n_gy + j

    def other_device(step):
        other = (place + step) % n_all
        return (other // n_gy, other % n_gy)

    lax.fori_loop(1, n_all, lambda step, carry: (greet(other_device(step)), carry)[1], 0)

    operands = {}
    for index, (name, source, target) in enumerate(
        (
            ("coarse", coarse_hbm, coarse_ref),
            ("map", map_hbm, map_ref),
            ("rhs", rhs_hbm, rhs_ref),
            ("basis", basis_t_hbm, basis_t),
            ("rows", rows_hbm, rows_ref),
            ("weight", weight_hbm, weight_ref),
            ("inverse", inverse_hbm, inverse_ref),
            ("block", block_hbm, block_ref),
        )
    ):
        operands[name] = pltpu.make_async_copy(source, target, operand_sem.at[index])
        operands[name].start()

    faces = (
        ((i - 1, j), i > 0, 1),
        ((i + 1, j), i < n_gx - 1, 0),
        ((i, j - 1), j > 0, 3),
        ((i, j + 1), j < n_gy - 1, 2),
    )

    for face, (_, present, _) in enumerate(faces):

        @pl.when(jnp.logical_not(present))
        def _():
            for exchange in range(margins.shape[0]):
                margins[exchange, face] = jnp.zeros(margins.shape[2:], BF16)
            for which in range(solved_margins.shape[0]):
                solved_margins[which, face] = jnp.zeros(solved_margins.shape[2:], BF16)
            basis_margins[face] = jnp.zeros(basis_margins.shape[1:], BF16)

    def start_copy(source, target, sends, recvs, device):
        pltpu.make_async_remote_copy(
            src_ref=source,
            dst_ref=target,
            send_sem=sends,
            recv_sem=recvs,
            device_id=device,
            device_id_type=MESH,
        ).start()

    def wait_bytes(ref, sem):
        pltpu.make_async_copy(ref, ref, sem).wait()

    def line_gather(slots, sems):
        def send(step):
            device = line_device((line + step) % n_line)
            start_copy(slots.at[line], slots.at[line], sems.at[0], sems.at[1], device)

        repeat(1, n_line, send)

    def plane_scatter(sources, slots, sems):
        def send(step):
            other = (spot + step) % n_plane
            start_copy(
                sources.at[other], slots.at[spot], sems.at[0], sems.at[1], plane_device(other)
            )

        repeat(1, n_plane, send)

    def wait_line(slots, sems, which):
        if n_line > 1:
            wait_bytes(slots.at[pl.ds(0, n_line - 1)], sems.at[which])

    def wait_plane(slots, sems, which):
        if n_plane > 1:
            wait_bytes(slots.at[pl.ds(0, n_plane - 1)], sems.at[which])

    def tile_of(sums, rows=8):
        rest = jnp.zeros((rows - len(sums), columns), F32)
        return jnp.concatenate(list(sums) + [rest], axis=0)

    def turn(chunk):
        start = chunk * LANES
        if not isinstance(start, int):
            start = pl.multiple_of(start, LANES)
        turned = coarse_ref[:, pl.ds(start, LANES)].astype(F32).T
        count = LANES // width
        coarse_t[pl.ds(chunk * count, count)] = turned.reshape(count, width, width)

    def arrange(member):
        parts = []
        for other_line in range(n_line):
            parts.append(coarse_t[map_ref[other_line * n_plane + member]])
        pieces[member] = jnp.concatenate(parts, axis=0).T.astype(BF16)

    def make_packs(exchange, rounded):
        packs[exchange] = (
            dot(select[...].reshape(-1, owned), rounded)
            .astype(BF16)
            .reshape(packs.shape[1:])
        )

    def send_faces(sources, targets, sends, recvs):
        for face, (device, present, block) in enumerate(faces):

            @pl.when(present)
            def _():
                start_copy(
                    sources[face], targets.at[block], sends.at[face], recvs.at[block], device
                )

    def wait_faces(targets, sems):
        for face, (_, present, _) in enumerate(faces):

            @pl.when(present)
            def _():
                wait_bytes(targets.at[face], sems.at[face])

    def send_packs(exchange):
        send_faces(
            [packs.at[exchange, face] for face in range(4)],
            margins.at[exchange],
            margin_send.at[exchange],
            margin_recv.at[exchange],
        )

    def wait_margins(exchange):
        wait_faces(margins.at[exchange], margin_recv.at[exchange])

    def store_line(which, parts, sums):
        gathered[which, line] = joined(dot(basis_t[...], parts)).astype(BF16)
        line_sums[which, line] = tile_of(sums)

    def send_line(which):
        line_gather(gathered.at[which], gather_sem.at[which])
        line_gather(line_sums.at[which], line_sem.at[which])

    def fold_basis():
        wait_faces(basis_margins, basis_recv)
        folds = []
        for face in range(4):
            folds.append(
                sum(
                    lax.dot_general(
                        spread[part, face],
                        basis_margins[face],
                        (((1,), (1,)), ((), ())),
                        preferred_element_type=F32,
                    )
                    for part in range(2)
                )
            )
        fold[...] = halves(jnp.concatenate(folds, axis=1))

    def apply_both(which, parts):
        local = joined(dot(inverse_ref[:, :owned], parts))
        wait_line(gathered.at[which], gather_sem.at[which], 1)
        products = dot(
            solver[...].reshape(n_plane * width, n_line * width),
            gathered[which].reshape(n_line * width, columns),
        ).reshape(n_plane, width, columns)
        partial[which, :, :width, :] = products
        wait_line(line_sums.at[which], line_sem.at[which], 1)
        line_total = jnp.sum(line_sums[which], axis=0)
        for member in range(n_plane):
            partial[which, member, width:, :] = line_total
        plane_scatter(partial.at[which], received.at[which], partial_sem.at[which])
        received[which, spot] = partial[which, spot]
        wait_margins(2 * which)
        local += dot(inverse_ref[:, owned:], margins[2 * which].reshape(-1, columns))
        make_packs(2 * which + 1, local.astype(BF16))
        send_packs(2 * which + 1)
        if which == 0:
            fold_basis()
        wait_plane(received.at[which], partial_sem.at[which], 1)
        total = jnp.sum(received[which], axis=0)
        solved[which] = total[:width].astype(BF16)
        send_faces(
            [solved.at[which]] * 4,
            solved_margins.at[which],
            solved_send.at[which],
            solved_recv.at[which],
        )
        applied = local + joined(dot(basis_ref[...], halves(total[:width])))
        halved = halves(applied)
        size = block_ref.shape[1]
        own = [
            joined(dot(block_ref[block], halved[block * size : (block + 1) * size]))
            for block in range(block_ref.shape[0])
        ]
        own = own[0] if len(own) == 1 else jnp.concatenate(own, axis=0)
        wait_margins(2 * which + 1)
        for face in range(4):
            margin = margins[2 * which + 1, face]
            own -= dot(spread[0, face], margin) + dot(spread[1, face], margin)
        wait_faces(solved_margins.at[which], solved_recv.at[which])
        coarse = solved_margins[which].reshape(4 * width, columns)
        own -= dot(fold[...], jnp.concatenate([coarse, coarse], axis=0))
        return applied, own, total[width:]

    operands["coarse"].wait()
    operands["map"].wait()
    repeat(0, coarse_ref.shape[1] // LANES, turn)
    repeat(0, n_plane, arrange)
    operands["rhs"].wait()
    operands["basis"].wait()
    right_side = rhs_ref[...]
    basis_ref[...] = basis_t[...].astype(F32).T.astype(BF16)
    parts = halves(right_side)
    store_line(0, parts, [column_sum(right_side * right_side)])
    operands["rows"].wait()
    operands["weight"].wait()
    row_ids = lax.broadcasted_iota(jnp.int32, (owned, rows_ref.shape[1]), 0)
    for face in range(4):
        hit = row_ids == rows_ref[face : face + 1, :]
        one_hot = jnp.where(hit, 1.0, 0.0).astype(F32)
        select[face] = one_hot.T.astype(BF16)
        basis_packs[face] = dot(basis_t[...], one_hot.astype(BF16)).astype(BF16)
        weights = jnp.where(hit, weight_ref[face : face + 1, :], 0.0)
        high = weights.astype(BF16)
        spread[0, face] = high
        spread[1, face] = (weights - high.astype(F32)).astype(BF16)
    make_packs(0, right_side.astype(BF16))

    pl.semaphore_wait(barrier, n_all - 1)
    plane_scatter(pieces, solver, pieces_sem)
    send_line(0)
    send_packs(0)
    send_faces(
        [basis_packs.at[face] for face in range(4)], basis_margins, basis_send, basis_recv
    )
    solver[spot] = pieces[spot]
    operands["inverse"].wait()
    operands["block"].wait()
    wait_plane(solver, pieces_sem, 1)

    applied, image, sums = apply_both(0, parts)
    rhs_square = sums[0:1]
    beta = jnp.sqrt(rhs_square + EPSILON)
    one_one = rhs_square / (rhs_square + EPSILON)
    krylov_one = right_side / beta
    image_one = image / beta

    parts = halves(image_one)
    store_line(
        1, parts, [column_sum(image_one * krylov_one), column_sum(image_one * image_one)]
    )
    send_line(1)
    make_packs(2, image_one.astype(BF16))
    send_packs(2)
    precond_one = applied / beta
    applied, image, sums = apply_both(1, parts)
    first_dot, image_square = sums[0:1], sums[1:2]
    remainder_square = image_square + first_dot * first_dot * (one_one - 2.0)
    remainder_square = jnp.maximum(remainder_square, 0.0)
    first_norm = jnp.sqrt(remainder_square + EPSILON)
    precond_two = (applied - first_dot * precond_one) / first_norm

    krylov_two = (image_one - first_dot * krylov_one) / first_norm
    one_two = first_dot * (1.0 - one_one) / first_norm
    two_two = remainder_square / (remainder_square + EPSILON)
    image = (image - first_dot * image_one) / first_norm
    all_sums[place] = tile_of(
        [
            column_sum(image * krylov_one),
            column_sum(image * krylov_two),
            column_sum(image * image),
        ],
        4,
    )

    def send_sums(step):
        start_copy(
            all_sums.at[place], all_sums.at[place], all_sem.at[0], all_sem.at[1], other_device(step)
        )

    repeat(1, n_all, send_sums, 32)
    wait_bytes(all_sums.at[pl.ds(0, n_all - 1)], all_sem.at[1])
    sums = jnp.sum(all_sums[...], axis=0)
    cross_dot, second_dot, image_square = sums[0:1], sums[1:2], sums[2:3]
    remainder_square = (
        image_square
        + cross_dot * cross_dot * (one_one - 2.0)
        + second_dot * second_dot * (two_two - 2.0)
        + 2.0 * cross_dot * second_dot * one_two
    )
    second_norm = jnp.sqrt(jnp.maximum(remainder_square, 0.0) + EPSILON)
    weight_one, weight_two, relative = least_squares(
        beta, first_dot, first_norm, cross_dot, second_dot, second_norm
    )
    out_ref[...] = weight_one * precond_one + weight_two * precond_two
    relative_ref[...] = relative

    for which in range(2):
        wait_line(line_sums.at[which], line_sem.at[which], 0)
    wait_bytes(all_sums.at[pl.ds(0, n_all - 1)], all_sem.at[0])
    wait_plane(solver, pieces_sem, 0)
    for which in range(2):
        wait_line(gathered.at[which], gather_sem.at[which], 0)
        wait_plane(received.at[which], partial_sem.at[which], 0)
    for exchange in range(4):
        for face, (_, present, _) in enumerate(faces):

            @pl.when(present)
            def _():
                wait_bytes(packs.at[exchange, face], margin_send.at[exchange, face])

    wait_faces(basis_packs, basis_send)
    for which in range(2):
        wait_faces(solved_margins.at[which], solved_send.at[which])


def on_device(
    n_gx,
    n_gy,
    rhs,
    face_rows,
    margin_weight,
    local_blocks,
    subdomain_inverse,
    coarse_basis,
    coarse_inverse,
    coarse_map,
):
    plane = 4 if n_gx % 4 == 0 else 1
    n_line, n_plane = n_gx // plane, plane * n_gy
    owned, columns = rhs.shape[2:]
    margin_rows = face_rows.shape[3]
    width = coarse_basis.shape[3]
    n_coarse = coarse_inverse.shape[3]
    vmem = pl.BlockSpec(memory_space=pltpu.VMEM)
    operands = (
        rhs[0, 0],
        face_rows[0, 0],
        margin_weight[0, 0],
        local_blocks[0, 0],
        subdomain_inverse[0, 0],
        coarse_basis[0, 0].T,
        coarse_inverse[0, 0],
        coarse_map,
    )
    dma = pltpu.SemaphoreType.DMA
    result, relative = pl.pallas_call(
        functools.partial(kernel, n_gx, n_gy, plane),
        out_shape=(
            jax.ShapeDtypeStruct((owned, columns), F32),
            jax.ShapeDtypeStruct((1, columns), F32),
        ),
        in_specs=[pl.BlockSpec(memory_space=pl.ANY)] * len(operands),
        out_specs=(vmem, vmem),
        scratch_shapes=[pltpu.VMEM(each.shape, each.dtype) for each in operands[:-1]]
        + [
            pltpu.SMEM(coarse_map.shape, coarse_map.dtype),
            pltpu.VMEM((n_coarse // width, width, width), F32),
            pltpu.VMEM((n_plane, width, n_line * width), BF16),
            pltpu.VMEM((n_plane, width, n_line * width), BF16),
            pltpu.VMEM((4, margin_rows, owned), BF16),
            pltpu.VMEM((2, 4, owned, margin_rows), BF16),
            pltpu.VMEM((owned, width), BF16),
            pltpu.VMEM((4, 4, margin_rows, columns), BF16),
            pltpu.VMEM((4, 4, margin_rows, columns), BF16),
            pltpu.VMEM((2, n_line, width, columns), BF16),
            pltpu.VMEM((2, n_plane, width + 8, columns), F32),
            pltpu.VMEM((2, n_plane, width + 8, columns), F32),
            pltpu.VMEM((2, n_line, 8, columns), F32),
            pltpu.VMEM((n_gx * n_gy, 4, columns), F32),
            pltpu.VMEM((4, width, margin_rows), BF16),
            pltpu.VMEM((4, width, margin_rows), BF16),
            pltpu.VMEM((owned, 8 * width), BF16),
            pltpu.VMEM((2, width, columns), BF16),
            pltpu.VMEM((2, 4, width, columns), BF16),
            dma((len(operands),)),
            dma((4,)),
            dma((4,)),
            dma((2, 4)),
            dma((2, 4)),
            dma((2,)),
            dma((4, 4)),
            dma((4, 4)),
            dma((2, 2)),
            dma((2, 2)),
            dma((2, 2)),
            dma((2,)),
        ],
        compiler_params=pltpu.CompilerParams(
            collective_id=0, has_side_effects=True, vmem_limit_bytes=56 * 1024 * 1024
        ),
    )(*operands)
    return (result[None, None], relative[0])


def solution(mesh):
    return jax.shard_map(
        functools.partial(on_device, mesh.shape["gx"], mesh.shape["gy"]),
        mesh=mesh,
        in_specs=(
            P("gx", "gy", None, None),
            P("gx", "gy", None, None),
            P("gx", "gy", None, None),
            P("gx", "gy", None, None, None),
            P("gx", "gy", None, None),
            P("gx", "gy", None, None),
            P("gx", "gy", None, None),
            P(),
        ),
        out_specs=(P("gx", "gy", None, None), P()),
        check_vma=False,
    )
```

```python
import functools

import jax
import jax.numpy as jnp
from jax import lax
from jax.experimental import pallas as pl
from jax.experimental.pallas import tpu as pltpu
from jax.sharding import PartitionSpec as P

EPSILON = 1e-06
MESH = pl.DeviceIdType.MESH
F32 = jnp.float32
BF16 = jnp.bfloat16
LANES = 128


def least_squares(scale_norm, first_dot, first_norm, cross_dot, second_dot, second_norm):
    radius_one = jnp.sqrt(first_dot * first_dot + first_norm * first_norm)
    cosine_one = first_dot / radius_one
    sine_one = first_norm / radius_one
    upper_entry = cosine_one * cross_dot + sine_one * second_dot
    lower_entry = cosine_one * second_dot - sine_one * cross_dot
    radius_two = jnp.sqrt(lower_entry * lower_entry + second_norm * second_norm)
    cosine_two = lower_entry / radius_two
    sine_two = second_norm / radius_two
    weight_two = -cosine_two * sine_one * scale_norm / radius_two
    weight_one = (cosine_one * scale_norm - upper_entry * weight_two) / radius_one
    return (weight_one, weight_two, sine_one * sine_two)


def dot(left, right):
    return jnp.dot(left, right, preferred_element_type=F32)


def repeat(first, last, body, unrolled=8):
    if last - first <= unrolled:
        for index in range(first, last):
            body(index)
    else:
        lax.fori_loop(first, last, lambda index, carry: (body(index), carry)[1], 0)


def column_sum(values):
    return jnp.sum(values, axis=0, keepdims=True)


def halves(values):
    high = values.astype(BF16)
    low = (values - high.astype(F32)).astype(BF16)
    return jnp.concatenate([high, low], axis=1)


def joined(values):
    columns = values.shape[1] // 2
    return values[:, :columns] + values[:, columns:]


def kernel(
    n_gx,
    n_gy,
    plane,
    rhs_hbm,
    rows_hbm,
    weight_hbm,
    block_hbm,
    inverse_hbm,
    basis_t_hbm,
    coarse_hbm,
    map_hbm,
    out_ref,
    relative_ref,
    rhs_ref,
    rows_ref,
    weight_ref,
    block_ref,
    inverse_ref,
    basis_t,
    coarse_ref,
    map_ref,
    coarse_t,
    pieces,
    solver,
    select,
    spread,
    basis_ref,
    packs,
    margins,
    gathered,
    partial,
    received,
    line_sums,
    all_sums,
    basis_packs,
    basis_margins,
    fold,
    solved,
    solved_margins,
    operand_sem,
    basis_send,
    basis_recv,
    solved_send,
    solved_recv,
    pieces_sem,
    margin_send,
    margin_recv,
    gather_sem,
    partial_sem,
    line_sem,
    all_sem,
):
    i = lax.axis_index("gx")
    j = lax.axis_index("gy")
    n_line = n_gx // plane
    n_plane = plane * n_gy
    line = i // plane
    spot = (i % plane) * n_gy + j
    owned, columns = rhs_ref.shape
    width = basis_ref.shape[1]

    def line_device(slot):
        return (slot * plane + i % plane, j)

    def plane_device(slot):
        return (line * plane + slot // n_gy, slot % n_gy)

    barrier = pltpu.get_barrier_semaphore()

    def greet(device):
        pl.semaphore_signal(barrier, inc=1, device_id=device, device_id_type=MESH)

    n_all = n_gx * n_gy
    place = i * n_gy + j

    def other_device(step):
        other = (place + step) % n_all
        return (other // n_gy, other % n_gy)

    repeat(1, n_line, lambda step: greet(line_device((line + step) % n_line)))
    repeat(1, n_plane, lambda step: greet(plane_device((spot + step) % n_plane)))
    cross_down = jnp.logical_and(i % plane == 0, i > 0)
    cross_up = jnp.logical_and(i % plane == plane - 1, i < n_gx - 1)
    peers = n_line + n_plane - 2
    if plane > 1:
        peers += cross_down.astype(jnp.int32) + cross_up.astype(jnp.int32)

        @pl.when(cross_down)
        def _():
            greet((i - 1, j))

        @pl.when(cross_up)
        def _():
            greet((i + 1, j))

    operands = {}
    for index, (name, source, target) in enumerate(
        (
            ("rhs", rhs_hbm, rhs_ref),
            ("basis", basis_t_hbm, basis_t),
            ("coarse", coarse_hbm, coarse_ref),
            ("map", map_hbm, map_ref),
            ("rows", rows_hbm, rows_ref),
            ("weight", weight_hbm, weight_ref),
            ("inverse", inverse_hbm, inverse_ref),
            ("block", block_hbm, block_ref),
        )
    ):
        operands[name] = pltpu.make_async_copy(source, target, operand_sem.at[index])
        operands[name].start()

    faces = (
        ((i - 1, j), i > 0, 1),
        ((i + 1, j), i < n_gx - 1, 0),
        ((i, j - 1), j > 0, 3),
        ((i, j + 1), j < n_gy - 1, 2),
    )

    for face, (_, present, _) in enumerate(faces):

        @pl.when(jnp.logical_not(present))
        def _():
            for exchange in range(margins.shape[0]):
                margins[exchange, face] = jnp.zeros(margins.shape[2:], BF16)
            for which in range(solved_margins.shape[0]):
                solved_margins[which, face] = jnp.zeros(solved_margins.shape[2:], BF16)
            basis_margins[face] = jnp.zeros(basis_margins.shape[1:], BF16)

    def start_copy(source, target, sends, recvs, device):
        pltpu.make_async_remote_copy(
            src_ref=source,
            dst_ref=target,
            send_sem=sends,
            recv_sem=recvs,
            device_id=device,
            device_id_type=MESH,
        ).start()

    def wait_bytes(ref, sem):
        pltpu.make_async_copy(ref, ref, sem).wait()

    def line_gather(slots, sems):
        def send(step):
            device = line_device((line + step) % n_line)
            start_copy(slots.at[line], slots.at[line], sems.at[0], sems.at[1], device)

        repeat(1, n_line, send)

    def plane_scatter(sources, slots, sems):
        def send(step):
            other = (spot + step) % n_plane
            start_copy(
                sources.at[other], slots.at[spot], sems.at[0], sems.at[1], plane_device(other)
            )

        repeat(1, n_plane, send)

    def wait_line(slots, sems, which):
        if n_line > 1:
            wait_bytes(slots.at[pl.ds(0, n_line - 1)], sems.at[which])

    def wait_plane(slots, sems, which):
        if n_plane > 1:
            wait_bytes(slots.at[pl.ds(0, n_plane - 1)], sems.at[which])

    def tile_of(sums, rows=8):
        rest = jnp.zeros((rows - len(sums), columns), F32)
        return jnp.concatenate(list(sums) + [rest], axis=0)

    def turn(chunk):
        start = chunk * LANES
        if not isinstance(start, int):
            start = pl.multiple_of(start, LANES)
        turned = coarse_ref[:, pl.ds(start, LANES)].astype(F32).T
        count = LANES // width
        coarse_t[pl.ds(chunk * count, count)] = turned.reshape(count, width, width)

    def arrange(member):
        parts = []
        for other_line in range(n_line):
            parts.append(coarse_t[map_ref[other_line * n_plane + member]])
        pieces[member] = jnp.concatenate(parts, axis=0).T.astype(BF16)

    def make_packs(exchange, rounded):
        packs[exchange] = (
            dot(select[...].reshape(-1, owned), rounded)
            .astype(BF16)
            .reshape(packs.shape[1:])
        )

    def send_faces(sources, targets, sends, recvs):
        for face, (device, present, block) in enumerate(faces):

            @pl.when(present)
            def _():
                start_copy(
                    sources[face], targets.at[block], sends.at[face], recvs.at[block], device
                )

    def wait_faces(targets, sems):
        for face, (_, present, _) in enumerate(faces):

            @pl.when(present)
            def _():
                wait_bytes(targets.at[face], sems.at[face])

    def send_packs(exchange):
        send_faces(
            [packs.at[exchange, face] for face in range(4)],
            margins.at[exchange],
            margin_send.at[exchange],
            margin_recv.at[exchange],
        )

    def wait_margins(exchange):
        wait_faces(margins.at[exchange], margin_recv.at[exchange])

    def store_line(which, parts, sums):
        gathered[which, line] = joined(dot(basis_t[...], parts)).astype(BF16)
        line_sums[which, line] = tile_of(sums)

    def send_line(which):
        line_gather(gathered.at[which], gather_sem.at[which])
        line_gather(line_sums.at[which], line_sem.at[which])

    def fold_basis():
        wait_faces(basis_margins, basis_recv)
        folds = []
        for face in range(4):
            folds.append(
                sum(
                    lax.dot_general(
                        spread[part, face],
                        basis_margins[face],
                        (((1,), (1,)), ((), ())),
                        preferred_element_type=F32,
                    )
                    for part in range(2)
                )
            )
        fold[...] = halves(jnp.concatenate(folds, axis=1))

    def apply_both(which, parts):
        local = joined(dot(inverse_ref[:, :owned], parts))
        wait_line(gathered.at[which], gather_sem.at[which], 1)
        products = dot(
            solver[...].reshape(n_plane * width, n_line * width),
            gathered[which].reshape(n_line * width, columns),
        ).reshape(n_plane, width, columns)
        partial[which, :, :width, :] = products
        wait_line(line_sums.at[which], line_sem.at[which], 1)
        line_total = jnp.sum(line_sums[which], axis=0)
        for member in range(n_plane):
            partial[which, member, width:, :] = line_total
        plane_scatter(partial.at[which], received.at[which], partial_sem.at[which])
        received[which, spot] = partial[which, spot]
        wait_margins(2 * which)
        local += dot(inverse_ref[:, owned:], margins[2 * which].reshape(-1, columns))
        make_packs(2 * which + 1, local.astype(BF16))
        send_packs(2 * which + 1)
        if which == 0:
            fold_basis()
        wait_plane(received.at[which], partial_sem.at[which], 1)
        total = jnp.sum(received[which], axis=0)
        solved[which] = total[:width].astype(BF16)
        send_faces(
            [solved.at[which]] * 4,
            solved_margins.at[which],
            solved_send.at[which],
            solved_recv.at[which],
        )
        applied = local + joined(dot(basis_ref[...], halves(total[:width])))
        halved = halves(applied)
        size = block_ref.shape[1]
        own = [
            joined(dot(block_ref[block], halved[block * size : (block + 1) * size]))
            for block in range(block_ref.shape[0])
        ]
        own = own[0] if len(own) == 1 else jnp.concatenate(own, axis=0)
        wait_margins(2 * which + 1)
        for face in range(4):
            margin = margins[2 * which + 1, face]
            own -= dot(spread[0, face], margin) + dot(spread[1, face], margin)
        wait_faces(solved_margins.at[which], solved_recv.at[which])
        coarse = solved_margins[which].reshape(4 * width, columns)
        own -= dot(fold[...], jnp.concatenate([coarse, coarse], axis=0))
        return applied, own, total[width:]

    operands["rhs"].wait()
    operands["basis"].wait()
    right_side = rhs_ref[...]
    parts = halves(right_side)
    store_line(0, parts, [column_sum(right_side * right_side)])
    operands["coarse"].wait()
    operands["map"].wait()
    repeat(0, coarse_ref.shape[1] // LANES, turn)
    repeat(0, n_plane, arrange)
    pl.semaphore_wait(barrier, peers)
    send_line(0)
    plane_scatter(pieces, solver, pieces_sem)
    solver[spot] = pieces[spot]
    operands["rows"].wait()
    operands["weight"].wait()
    row_ids = lax.broadcasted_iota(jnp.int32, (owned, rows_ref.shape[1]), 0)
    for face in range(4):
        hit = row_ids == rows_ref[face : face + 1, :]
        one_hot = jnp.where(hit, 1.0, 0.0).astype(F32)
        select[face] = one_hot.T.astype(BF16)
        basis_packs[face] = dot(basis_t[...], one_hot.astype(BF16)).astype(BF16)
    make_packs(0, right_side.astype(BF16))
    send_packs(0)
    send_faces(
        [basis_packs.at[face] for face in range(4)], basis_margins, basis_send, basis_recv
    )
    for face in range(4):
        hit = row_ids == rows_ref[face : face + 1, :]
        weights = jnp.where(hit, weight_ref[face : face + 1, :], 0.0)
        high = weights.astype(BF16)
        spread[0, face] = high
        spread[1, face] = (weights - high.astype(F32)).astype(BF16)
    basis_ref[...] = basis_t[...].astype(F32).T.astype(BF16)
    operands["inverse"].wait()
    operands["block"].wait()
    wait_plane(solver, pieces_sem, 1)

    applied, image, sums = apply_both(0, parts)
    rhs_square = sums[0:1]
    beta = jnp.sqrt(rhs_square + EPSILON)
    one_one = rhs_square / (rhs_square + EPSILON)
    krylov_one = right_side / beta
    image_one = image / beta

    parts = halves(image_one)
    store_line(
        1, parts, [column_sum(image_one * krylov_one), column_sum(image_one * image_one)]
    )
    send_line(1)
    make_packs(2, image_one.astype(BF16))
    send_packs(2)
    precond_one = applied / beta
    applied, image, sums = apply_both(1, parts)
    first_dot, image_square = sums[0:1], sums[1:2]
    remainder_square = image_square + first_dot * first_dot * (one_one - 2.0)
    remainder_square = jnp.maximum(remainder_square, 0.0)
    first_norm = jnp.sqrt(remainder_square + EPSILON)
    precond_two = (applied - first_dot * precond_one) / first_norm

    krylov_two = (image_one - first_dot * krylov_one) / first_norm
    one_two = first_dot * (1.0 - one_one) / first_norm
    two_two = remainder_square / (remainder_square + EPSILON)
    image = (image - first_dot * image_one) / first_norm
    all_sums[place] = tile_of(
        [
            column_sum(image * krylov_one),
            column_sum(image * krylov_two),
            column_sum(image * image),
        ],
        4,
    )

    def send_sums(step):
        start_copy(
            all_sums.at[place], all_sums.at[place], all_sem.at[0], all_sem.at[1], other_device(step)
        )

    repeat(1, n_all, send_sums, 32)
    wait_bytes(all_sums.at[pl.ds(0, n_all - 1)], all_sem.at[1])
    sums = jnp.sum(all_sums[...], axis=0)
    cross_dot, second_dot, image_square = sums[0:1], sums[1:2], sums[2:3]
    remainder_square = (
        image_square
        + cross_dot * cross_dot * (one_one - 2.0)
        + second_dot * second_dot * (two_two - 2.0)
        + 2.0 * cross_dot * second_dot * one_two
    )
    second_norm = jnp.sqrt(jnp.maximum(remainder_square, 0.0) + EPSILON)
    weight_one, weight_two, relative = least_squares(
        beta, first_dot, first_norm, cross_dot, second_dot, second_norm
    )
    out_ref[...] = weight_one * precond_one + weight_two * precond_two
    relative_ref[...] = relative

    for which in range(2):
        wait_line(line_sums.at[which], line_sem.at[which], 0)
    wait_bytes(all_sums.at[pl.ds(0, n_all - 1)], all_sem.at[0])
    wait_plane(solver, pieces_sem, 0)
    for which in range(2):
        wait_line(gathered.at[which], gather_sem.at[which], 0)
        wait_plane(received.at[which], partial_sem.at[which], 0)
    for exchange in range(4):
        for face, (_, present, _) in enumerate(faces):

            @pl.when(present)
            def _():
                wait_bytes(packs.at[exchange, face], margin_send.at[exchange, face])

    wait_faces(basis_packs, basis_send)
    for which in range(2):
        wait_faces(solved_margins.at[which], solved_send.at[which])


def on_device(
    n_gx,
    n_gy,
    rhs,
    face_rows,
    margin_weight,
    local_blocks,
    subdomain_inverse,
    coarse_basis,
    coarse_inverse,
    coarse_map,
):
    plane = 4 if n_gx % 4 == 0 else 1
    n_line, n_plane = n_gx // plane, plane * n_gy
    owned, columns = rhs.shape[2:]
    margin_rows = face_rows.shape[3]
    width = coarse_basis.shape[3]
    n_coarse = coarse_inverse.shape[3]
    vmem = pl.BlockSpec(memory_space=pltpu.VMEM)
    operands = (
        rhs[0, 0],
        face_rows[0, 0],
        margin_weight[0, 0],
        local_blocks[0, 0],
        subdomain_inverse[0, 0],
        coarse_basis[0, 0].T,
        coarse_inverse[0, 0],
        coarse_map,
    )
    dma = pltpu.SemaphoreType.DMA
    result, relative = pl.pallas_call(
        functools.partial(kernel, n_gx, n_gy, plane),
        out_shape=(
            jax.ShapeDtypeStruct((owned, columns), F32),
            jax.ShapeDtypeStruct((1, columns), F32),
        ),
        in_specs=[pl.BlockSpec(memory_space=pl.ANY)] * len(operands),
        out_specs=(vmem, vmem),
        scratch_shapes=[pltpu.VMEM(each.shape, each.dtype) for each in operands[:-1]]
        + [
            pltpu.SMEM(coarse_map.shape, coarse_map.dtype),
            pltpu.VMEM((n_coarse // width, width, width), F32),
            pltpu.VMEM((n_plane, width, n_line * width), BF16),
            pltpu.VMEM((n_plane, width, n_line * width), BF16),
            pltpu.VMEM((4, margin_rows, owned), BF16),
            pltpu.VMEM((2, 4, owned, margin_rows), BF16),
            pltpu.VMEM((owned, width), BF16),
            pltpu.VMEM((4, 4, margin_rows, columns), BF16),
            pltpu.VMEM((4, 4, margin_rows, columns), BF16),
            pltpu.VMEM((2, n_line, width, columns), BF16),
            pltpu.VMEM((2, n_plane, width + 8, columns), F32),
            pltpu.VMEM((2, n_plane, width + 8, columns), F32),
            pltpu.VMEM((2, n_line, 8, columns), F32),
            pltpu.VMEM((n_gx * n_gy, 4, columns), F32),
            pltpu.VMEM((4, width, margin_rows), BF16),
            pltpu.VMEM((4, width, margin_rows), BF16),
            pltpu.VMEM((owned, 8 * width), BF16),
            pltpu.VMEM((2, width, columns), BF16),
            pltpu.VMEM((2, 4, width, columns), BF16),
            dma((len(operands),)),
            dma((4,)),
            dma((4,)),
            dma((2, 4)),
            dma((2, 4)),
            dma((2,)),
            dma((4, 4)),
            dma((4, 4)),
            dma((2, 2)),
            dma((2, 2)),
            dma((2, 2)),
            dma((2,)),
        ],
        compiler_params=pltpu.CompilerParams(
            collective_id=0, has_side_effects=True, vmem_limit_bytes=56 * 1024 * 1024
        ),
    )(*operands)
    return (result[None, None], relative[0])


def solution(mesh):
    return jax.shard_map(
        functools.partial(on_device, mesh.shape["gx"], mesh.shape["gy"]),
        mesh=mesh,
        in_specs=(
            P("gx", "gy", None, None),
            P("gx", "gy", None, None),
            P("gx", "gy", None, None),
            P("gx", "gy", None, None, None),
            P("gx", "gy", None, None),
            P("gx", "gy", None, None),
            P("gx", "gy", None, None),
            P(),
        ),
        out_specs=(P("gx", "gy", None, None), P()),
        check_vma=False,
    )
```

```python
import functools

import jax
import jax.numpy as jnp
from jax import lax
from jax.experimental import pallas as pl
from jax.experimental.pallas import tpu as pltpu
from jax.sharding import PartitionSpec as P

EPSILON = 1e-06
MESH = pl.DeviceIdType.MESH
F32 = jnp.float32
BF16 = jnp.bfloat16
LANES = 128


def least_squares(scale_norm, first_dot, first_norm, cross_dot, second_dot, second_norm):
    radius_one = jnp.sqrt(first_dot * first_dot + first_norm * first_norm)
    cosine_one = first_dot / radius_one
    sine_one = first_norm / radius_one
    upper_entry = cosine_one * cross_dot + sine_one * second_dot
    lower_entry = cosine_one * second_dot - sine_one * cross_dot
    radius_two = jnp.sqrt(lower_entry * lower_entry + second_norm * second_norm)
    cosine_two = lower_entry / radius_two
    sine_two = second_norm / radius_two
    weight_two = -cosine_two * sine_one * scale_norm / radius_two
    weight_one = (cosine_one * scale_norm - upper_entry * weight_two) / radius_one
    return (weight_one, weight_two, sine_one * sine_two)


def dot(left, right):
    return jnp.dot(left, right, preferred_element_type=F32)


def repeat(first, last, body, unrolled=8):
    if last - first <= unrolled:
        for index in range(first, last):
            body(index)
    else:
        lax.fori_loop(first, last, lambda index, carry: (body(index), carry)[1], 0)


def column_sum(values):
    return jnp.sum(values, axis=0, keepdims=True)


def halves(values):
    high = values.astype(BF16)
    low = (values - high.astype(F32)).astype(BF16)
    return jnp.concatenate([high, low], axis=1)


def joined(values):
    columns = values.shape[1] // 2
    return values[:, :columns] + values[:, columns:]


def kernel(
    n_gx,
    n_gy,
    plane,
    rhs_hbm,
    rows_hbm,
    weight_hbm,
    block_hbm,
    inverse_hbm,
    basis_t_hbm,
    coarse_hbm,
    map_hbm,
    out_ref,
    relative_ref,
    rhs_ref,
    rows_ref,
    weight_ref,
    block_ref,
    inverse_ref,
    basis_t,
    coarse_ref,
    map_ref,
    coarse_t,
    pieces,
    solver,
    select,
    spread,
    basis_ref,
    packs,
    margins,
    gathered,
    partial,
    received,
    line_sums,
    all_sums,
    basis_packs,
    basis_margins,
    fold,
    solved,
    solved_margins,
    operand_sem,
    basis_send,
    basis_recv,
    solved_send,
    solved_recv,
    pieces_sem,
    margin_send,
    margin_recv,
    gather_sem,
    partial_sem,
    line_sem,
    all_sem,
):
    i = lax.axis_index("gx")
    j = lax.axis_index("gy")
    n_line = n_gx // plane
    n_plane = plane * n_gy
    line = i // plane
    spot = (i % plane) * n_gy + j
    owned, columns = rhs_ref.shape
    width = basis_ref.shape[1]

    def line_device(slot):
        return (slot * plane + i % plane, j)

    def plane_device(slot):
        return (line * plane + slot // n_gy, slot % n_gy)

    barrier = pltpu.get_barrier_semaphore()

    def greet(device):
        pl.semaphore_signal(barrier, inc=1, device_id=device, device_id_type=MESH)

    n_all = n_gx * n_gy
    place = i * n_gy + j

    def other_device(step):
        other = (place + step) % n_all
        return (other // n_gy, other % n_gy)

    repeat(1, n_line, lambda step: greet(line_device((line + step) % n_line)))
    repeat(1, n_plane, lambda step: greet(plane_device((spot + step) % n_plane)))
    cross_down = jnp.logical_and(i % plane == 0, i > 0)
    cross_up = jnp.logical_and(i % plane == plane - 1, i < n_gx - 1)
    peers = n_line + n_plane - 2
    if plane > 1:
        peers += cross_down.astype(jnp.int32) + cross_up.astype(jnp.int32)

        @pl.when(cross_down)
        def _():
            greet((i - 1, j))

        @pl.when(cross_up)
        def _():
            greet((i + 1, j))

    operands = {}
    for index, (name, source, target) in enumerate(
        (
            ("rhs", rhs_hbm, rhs_ref),
            ("basis", basis_t_hbm, basis_t),
            ("coarse", coarse_hbm, coarse_ref),
            ("map", map_hbm, map_ref),
            ("rows", rows_hbm, rows_ref),
            ("weight", weight_hbm, weight_ref),
            ("inverse", inverse_hbm, inverse_ref),
            ("block", block_hbm, block_ref),
        )
    ):
        operands[name] = pltpu.make_async_copy(source, target, operand_sem.at[index])
        operands[name].start()

    faces = (
        ((i - 1, j), i > 0, 1),
        ((i + 1, j), i < n_gx - 1, 0),
        ((i, j - 1), j > 0, 3),
        ((i, j + 1), j < n_gy - 1, 2),
    )

    for face, (_, present, _) in enumerate(faces):

        @pl.when(jnp.logical_not(present))
        def _():
            for exchange in range(margins.shape[0]):
                margins[exchange, face] = jnp.zeros(margins.shape[2:], BF16)
            for which in range(solved_margins.shape[0]):
                solved_margins[which, face] = jnp.zeros(solved_margins.shape[2:], BF16)
            basis_margins[face] = jnp.zeros(basis_margins.shape[1:], BF16)

    def start_copy(source, target, sends, recvs, device):
        pltpu.make_async_remote_copy(
            src_ref=source,
            dst_ref=target,
            send_sem=sends,
            recv_sem=recvs,
            device_id=device,
            device_id_type=MESH,
        ).start()

    def wait_bytes(ref, sem):
        pltpu.make_async_copy(ref, ref, sem).wait()

    def line_gather(slots, sems):
        def send(step):
            device = line_device((line + step) % n_line)
            start_copy(slots.at[line], slots.at[line], sems.at[0], sems.at[1], device)

        repeat(1, n_line, send)

    def plane_scatter(sources, slots, sems):
        def send(step):
            other = (spot + step) % n_plane
            start_copy(
                sources.at[other], slots.at[spot], sems.at[0], sems.at[1], plane_device(other)
            )

        repeat(1, n_plane, send)

    def wait_line(slots, sems, which):
        if n_line > 1:
            wait_bytes(slots.at[pl.ds(0, n_line - 1)], sems.at[which])

    def wait_plane(slots, sems, which):
        if n_plane > 1:
            wait_bytes(slots.at[pl.ds(0, n_plane - 1)], sems.at[which])

    def tile_of(sums, rows=8):
        rest = jnp.zeros((rows - len(sums), columns), F32)
        return jnp.concatenate(list(sums) + [rest], axis=0)

    def turn(chunk):
        start = chunk * LANES
        if not isinstance(start, int):
            start = pl.multiple_of(start, LANES)
        turned = coarse_ref[:, pl.ds(start, LANES)].astype(F32).T
        count = LANES // width
        coarse_t[pl.ds(chunk * count, count)] = turned.reshape(count, width, width)

    def arrange(member):
        parts = []
        for other_line in range(n_line):
            parts.append(coarse_t[map_ref[other_line * n_plane + member]])
        pieces[member] = jnp.concatenate(parts, axis=0).T.astype(BF16)

    def make_packs(exchange, rounded):
        packs[exchange] = (
            dot(select[...].reshape(-1, owned), rounded)
            .astype(BF16)
            .reshape(packs.shape[1:])
        )

    def send_faces(sources, targets, sends, recvs):
        for face, (device, present, block) in enumerate(faces):

            @pl.when(present)
            def _():
                start_copy(
                    sources[face], targets.at[block], sends.at[face], recvs.at[block], device
                )

    def wait_faces(targets, sems):
        for face, (_, present, _) in enumerate(faces):

            @pl.when(present)
            def _():
                wait_bytes(targets.at[face], sems.at[face])

    def send_packs(exchange):
        send_faces(
            [packs.at[exchange, face] for face in range(4)],
            margins.at[exchange],
            margin_send.at[exchange],
            margin_recv.at[exchange],
        )

    def wait_margins(exchange):
        wait_faces(margins.at[exchange], margin_recv.at[exchange])

    def store_line(which, parts, sums):
        gathered[which, line] = joined(dot(basis_t[...], parts)).astype(BF16)
        line_sums[which, line] = tile_of(sums)

    def send_line(which):
        line_gather(gathered.at[which], gather_sem.at[which])
        line_gather(line_sums.at[which], line_sem.at[which])

    def fold_basis():
        wait_faces(basis_margins, basis_recv)
        folds = []
        for face in range(4):
            folds.append(
                sum(
                    lax.dot_general(
                        spread[part, face],
                        basis_margins[face],
                        (((1,), (1,)), ((), ())),
                        preferred_element_type=F32,
                    )
                    for part in range(2)
                )
            )
        fold[...] = halves(jnp.concatenate(folds, axis=1))

    def apply_both(which, parts):
        local = joined(dot(inverse_ref[:, :owned], parts))
        wait_line(gathered.at[which], gather_sem.at[which], 1)
        products = dot(
            solver[...].reshape(n_plane * width, n_line * width),
            gathered[which].reshape(n_line * width, columns),
        ).reshape(n_plane, width, columns)
        partial[which, :, :width, :] = products.astype(BF16)
        wait_line(line_sums.at[which], line_sem.at[which], 1)
        line_total = jnp.sum(line_sums[which], axis=0)[:4]
        high = line_total.astype(BF16).astype(F32)
        middle = (line_total - high).astype(BF16).astype(F32)
        low = line_total - high - middle
        packed = jnp.concatenate([high, middle, low, jnp.zeros_like(low)], axis=0).astype(BF16)
        for member in range(n_plane):
            partial[which, member, width:, :] = packed
        plane_scatter(partial.at[which], received.at[which], partial_sem.at[which])
        received[which, spot] = partial[which, spot]
        wait_margins(2 * which)
        local += dot(inverse_ref[:, owned:], margins[2 * which].reshape(-1, columns))
        make_packs(2 * which + 1, local.astype(BF16))
        send_packs(2 * which + 1)
        if which == 0:
            fold_basis()
        wait_plane(received.at[which], partial_sem.at[which], 1)
        total = jnp.sum(received[which].astype(F32), axis=0)
        packed = total[width:]
        solved[which] = total[:width].astype(BF16)
        send_faces(
            [solved.at[which]] * 4,
            solved_margins.at[which],
            solved_send.at[which],
            solved_recv.at[which],
        )
        applied = local + joined(dot(basis_ref[...], halves(total[:width])))
        halved = halves(applied)
        size = block_ref.shape[1]
        own = [
            joined(dot(block_ref[block], halved[block * size : (block + 1) * size]))
            for block in range(block_ref.shape[0])
        ]
        own = own[0] if len(own) == 1 else jnp.concatenate(own, axis=0)
        wait_margins(2 * which + 1)
        for face in range(4):
            margin = margins[2 * which + 1, face]
            own -= dot(spread[0, face], margin) + dot(spread[1, face], margin)
        wait_faces(solved_margins.at[which], solved_recv.at[which])
        coarse = solved_margins[which].reshape(4 * width, columns)
        own -= dot(fold[...], jnp.concatenate([coarse, coarse], axis=0))
        return applied, own, packed[0:4] + packed[4:8] + packed[8:12]

    operands["rhs"].wait()
    operands["basis"].wait()
    right_side = rhs_ref[...]
    parts = halves(right_side)
    store_line(0, parts, [column_sum(right_side * right_side)])
    operands["coarse"].wait()
    operands["map"].wait()
    repeat(0, coarse_ref.shape[1] // LANES, turn)
    repeat(0, n_plane, arrange)
    pl.semaphore_wait(barrier, peers)
    send_line(0)
    plane_scatter(pieces, solver, pieces_sem)
    solver[spot] = pieces[spot]
    operands["rows"].wait()
    operands["weight"].wait()
    row_ids = lax.broadcasted_iota(jnp.int32, (owned, rows_ref.shape[1]), 0)
    for face in range(4):
        hit = row_ids == rows_ref[face : face + 1, :]
        one_hot = jnp.where(hit, 1.0, 0.0).astype(F32)
        select[face] = one_hot.T.astype(BF16)
        basis_packs[face] = dot(basis_t[...], one_hot.astype(BF16)).astype(BF16)
    make_packs(0, right_side.astype(BF16))
    send_packs(0)
    send_faces(
        [basis_packs.at[face] for face in range(4)], basis_margins, basis_send, basis_recv
    )
    for face in range(4):
        hit = row_ids == rows_ref[face : face + 1, :]
        weights = jnp.where(hit, weight_ref[face : face + 1, :], 0.0)
        high = weights.astype(BF16)
        spread[0, face] = high
        spread[1, face] = (weights - high.astype(F32)).astype(BF16)
    basis_ref[...] = basis_t[...].astype(F32).T.astype(BF16)
    operands["inverse"].wait()
    operands["block"].wait()
    wait_plane(solver, pieces_sem, 1)

    applied, image, sums = apply_both(0, parts)
    rhs_square = sums[0:1]
    beta = jnp.sqrt(rhs_square + EPSILON)
    one_one = rhs_square / (rhs_square + EPSILON)
    krylov_one = right_side / beta
    image_one = image / beta

    parts = halves(image_one)
    store_line(
        1, parts, [column_sum(image_one * krylov_one), column_sum(image_one * image_one)]
    )
    send_line(1)
    make_packs(2, image_one.astype(BF16))
    send_packs(2)
    precond_one = applied / beta
    applied, image, sums = apply_both(1, parts)
    first_dot, image_square = sums[0:1], sums[1:2]
    remainder_square = image_square + first_dot * first_dot * (one_one - 2.0)
    remainder_square = jnp.maximum(remainder_square, 0.0)
    first_norm = jnp.sqrt(remainder_square + EPSILON)
    precond_two = (applied - first_dot * precond_one) / first_norm

    krylov_two = (image_one - first_dot * krylov_one) / first_norm
    one_two = first_dot * (1.0 - one_one) / first_norm
    two_two = remainder_square / (remainder_square + EPSILON)
    image = (image - first_dot * image_one) / first_norm
    all_sums[place] = tile_of(
        [
            column_sum(image * krylov_one),
            column_sum(image * krylov_two),
            column_sum(image * image),
        ],
        4,
    )

    def send_sums(step):
        start_copy(
            all_sums.at[place], all_sums.at[place], all_sem.at[0], all_sem.at[1], other_device(step)
        )

    repeat(1, n_all, send_sums, 32)
    wait_bytes(all_sums.at[pl.ds(0, n_all - 1)], all_sem.at[1])
    sums = jnp.sum(all_sums[...], axis=0)
    cross_dot, second_dot, image_square = sums[0:1], sums[1:2], sums[2:3]
    remainder_square = (
        image_square
        + cross_dot * cross_dot * (one_one - 2.0)
        + second_dot * second_dot * (two_two - 2.0)
        + 2.0 * cross_dot * second_dot * one_two
    )
    second_norm = jnp.sqrt(jnp.maximum(remainder_square, 0.0) + EPSILON)
    weight_one, weight_two, relative = least_squares(
        beta, first_dot, first_norm, cross_dot, second_dot, second_norm
    )
    out_ref[...] = weight_one * precond_one + weight_two * precond_two
    relative_ref[...] = relative

    for which in range(2):
        wait_line(line_sums.at[which], line_sem.at[which], 0)
    wait_bytes(all_sums.at[pl.ds(0, n_all - 1)], all_sem.at[0])
    wait_plane(solver, pieces_sem, 0)
    for which in range(2):
        wait_line(gathered.at[which], gather_sem.at[which], 0)
        wait_plane(received.at[which], partial_sem.at[which], 0)
    for exchange in range(4):
        for face, (_, present, _) in enumerate(faces):

            @pl.when(present)
            def _():
                wait_bytes(packs.at[exchange, face], margin_send.at[exchange, face])

    wait_faces(basis_packs, basis_send)
    for which in range(2):
        wait_faces(solved_margins.at[which], solved_send.at[which])


def on_device(
    n_gx,
    n_gy,
    rhs,
    face_rows,
    margin_weight,
    local_blocks,
    subdomain_inverse,
    coarse_basis,
    coarse_inverse,
    coarse_map,
):
    plane = 4 if n_gx % 4 == 0 else 1
    n_line, n_plane = n_gx // plane, plane * n_gy
    owned, columns = rhs.shape[2:]
    margin_rows = face_rows.shape[3]
    width = coarse_basis.shape[3]
    n_coarse = coarse_inverse.shape[3]
    vmem = pl.BlockSpec(memory_space=pltpu.VMEM)
    operands = (
        rhs[0, 0],
        face_rows[0, 0],
        margin_weight[0, 0],
        local_blocks[0, 0],
        subdomain_inverse[0, 0],
        coarse_basis[0, 0].T,
        coarse_inverse[0, 0],
        coarse_map,
    )
    dma = pltpu.SemaphoreType.DMA
    result, relative = pl.pallas_call(
        functools.partial(kernel, n_gx, n_gy, plane),
        out_shape=(
            jax.ShapeDtypeStruct((owned, columns), F32),
            jax.ShapeDtypeStruct((1, columns), F32),
        ),
        in_specs=[pl.BlockSpec(memory_space=pl.ANY)] * len(operands),
        out_specs=(vmem, vmem),
        scratch_shapes=[pltpu.VMEM(each.shape, each.dtype) for each in operands[:-1]]
        + [
            pltpu.SMEM(coarse_map.shape, coarse_map.dtype),
            pltpu.VMEM((n_coarse // width, width, width), F32),
            pltpu.VMEM((n_plane, width, n_line * width), BF16),
            pltpu.VMEM((n_plane, width, n_line * width), BF16),
            pltpu.VMEM((4, margin_rows, owned), BF16),
            pltpu.VMEM((2, 4, owned, margin_rows), BF16),
            pltpu.VMEM((owned, width), BF16),
            pltpu.VMEM((4, 4, margin_rows, columns), BF16),
            pltpu.VMEM((4, 4, margin_rows, columns), BF16),
            pltpu.VMEM((2, n_line, width, columns), BF16),
            pltpu.VMEM((2, n_plane, width + 16, columns), BF16),
            pltpu.VMEM((2, n_plane, width + 16, columns), BF16),
            pltpu.VMEM((2, n_line, 8, columns), F32),
            pltpu.VMEM((n_gx * n_gy, 4, columns), F32),
            pltpu.VMEM((4, width, margin_rows), BF16),
            pltpu.VMEM((4, width, margin_rows), BF16),
            pltpu.VMEM((owned, 8 * width), BF16),
            pltpu.VMEM((2, width, columns), BF16),
            pltpu.VMEM((2, 4, width, columns), BF16),
            dma((len(operands),)),
            dma((4,)),
            dma((4,)),
            dma((2, 4)),
            dma((2, 4)),
            dma((2,)),
            dma((4, 4)),
            dma((4, 4)),
            dma((2, 2)),
            dma((2, 2)),
            dma((2, 2)),
            dma((2,)),
        ],
        compiler_params=pltpu.CompilerParams(
            collective_id=0, has_side_effects=True, vmem_limit_bytes=56 * 1024 * 1024
        ),
    )(*operands)
    return (result[None, None], relative[0])


def solution(mesh):
    return jax.shard_map(
        functools.partial(on_device, mesh.shape["gx"], mesh.shape["gy"]),
        mesh=mesh,
        in_specs=(
            P("gx", "gy", None, None),
            P("gx", "gy", None, None),
            P("gx", "gy", None, None),
            P("gx", "gy", None, None, None),
            P("gx", "gy", None, None),
            P("gx", "gy", None, None),
            P("gx", "gy", None, None),
            P(),
        ),
        out_specs=(P("gx", "gy", None, None), P()),
        check_vma=False,
    )
```

```python
import functools

import jax
import jax.numpy as jnp
from jax import lax
from jax.experimental import pallas as pl
from jax.experimental.pallas import tpu as pltpu
from jax.sharding import PartitionSpec as P

EPSILON = 1e-06
MESH = pl.DeviceIdType.MESH
F32 = jnp.float32
BF16 = jnp.bfloat16
LANES = 128


def least_squares(scale_norm, first_dot, first_norm, cross_dot, second_dot, second_norm):
    radius_one = jnp.sqrt(first_dot * first_dot + first_norm * first_norm)
    cosine_one = first_dot / radius_one
    sine_one = first_norm / radius_one
    upper_entry = cosine_one * cross_dot + sine_one * second_dot
    lower_entry = cosine_one * second_dot - sine_one * cross_dot
    radius_two = jnp.sqrt(lower_entry * lower_entry + second_norm * second_norm)
    cosine_two = lower_entry / radius_two
    sine_two = second_norm / radius_two
    weight_two = -cosine_two * sine_one * scale_norm / radius_two
    weight_one = (cosine_one * scale_norm - upper_entry * weight_two) / radius_one
    return (weight_one, weight_two, sine_one * sine_two)


def dot(left, right):
    return jnp.dot(left, right, preferred_element_type=F32)


def repeat(first, last, body, unrolled=8):
    if last - first <= unrolled:
        for index in range(first, last):
            body(index)
    else:
        lax.fori_loop(first, last, lambda index, carry: (body(index), carry)[1], 0)


def column_sum(values):
    return jnp.sum(values, axis=0, keepdims=True)


def halves(values):
    high = values.astype(BF16)
    low = (values - high.astype(F32)).astype(BF16)
    return jnp.concatenate([high, low], axis=1)


def joined(values):
    columns = values.shape[1] // 2
    return values[:, :columns] + values[:, columns:]


def kernel(
    n_gx,
    n_gy,
    plane,
    rhs_hbm,
    rows_hbm,
    weight_hbm,
    block_hbm,
    inverse_hbm,
    basis_t_hbm,
    coarse_hbm,
    map_hbm,
    out_ref,
    relative_ref,
    rhs_ref,
    rows_ref,
    weight_ref,
    block_ref,
    inverse_ref,
    basis_t,
    coarse_ref,
    map_ref,
    coarse_t,
    pieces,
    solver,
    select,
    spread,
    basis_ref,
    packs,
    margins,
    gathered,
    partial,
    received,
    all_sums,
    basis_packs,
    basis_margins,
    fold,
    solved,
    solved_margins,
    operand_sem,
    basis_send,
    basis_recv,
    solved_send,
    solved_recv,
    pieces_sem,
    margin_send,
    margin_recv,
    gather_sem,
    partial_sem,
    all_sem,
):
    i = lax.axis_index("gx")
    j = lax.axis_index("gy")
    n_line = n_gx // plane
    n_plane = plane * n_gy
    line = i // plane
    spot = (i % plane) * n_gy + j
    owned, columns = rhs_ref.shape
    width = basis_ref.shape[1]

    def line_device(slot):
        return (slot * plane + i % plane, j)

    def plane_device(slot):
        return (line * plane + slot // n_gy, slot % n_gy)

    barrier = pltpu.get_barrier_semaphore()

    def greet(device):
        pl.semaphore_signal(barrier, inc=1, device_id=device, device_id_type=MESH)

    n_all = n_gx * n_gy
    place = i * n_gy + j

    def other_device(step):
        other = (place + step) % n_all
        return (other // n_gy, other % n_gy)

    repeat(1, n_line, lambda step: greet(line_device((line + step) % n_line)))
    repeat(1, n_plane, lambda step: greet(plane_device((spot + step) % n_plane)))
    cross_down = jnp.logical_and(i % plane == 0, i > 0)
    cross_up = jnp.logical_and(i % plane == plane - 1, i < n_gx - 1)
    peers = n_line + n_plane - 2
    if plane > 1:
        peers += cross_down.astype(jnp.int32) + cross_up.astype(jnp.int32)

        @pl.when(cross_down)
        def _():
            greet((i - 1, j))

        @pl.when(cross_up)
        def _():
            greet((i + 1, j))

    operands = {}
    for index, (name, source, target) in enumerate(
        (
            ("rhs", rhs_hbm, rhs_ref),
            ("basis", basis_t_hbm, basis_t),
            ("coarse", coarse_hbm, coarse_ref),
            ("map", map_hbm, map_ref),
            ("rows", rows_hbm, rows_ref),
            ("weight", weight_hbm, weight_ref),
            ("inverse", inverse_hbm, inverse_ref),
            ("block", block_hbm, block_ref),
        )
    ):
        operands[name] = pltpu.make_async_copy(source, target, operand_sem.at[index])
        operands[name].start()

    faces = (
        ((i - 1, j), i > 0, 1),
        ((i + 1, j), i < n_gx - 1, 0),
        ((i, j - 1), j > 0, 3),
        ((i, j + 1), j < n_gy - 1, 2),
    )

    for face, (_, present, _) in enumerate(faces):

        @pl.when(jnp.logical_not(present))
        def _():
            for exchange in range(margins.shape[0]):
                margins[exchange, face] = jnp.zeros(margins.shape[2:], BF16)
            for which in range(solved_margins.shape[0]):
                solved_margins[which, face] = jnp.zeros(solved_margins.shape[2:], BF16)
            basis_margins[face] = jnp.zeros(basis_margins.shape[1:], BF16)

    def start_copy(source, target, sends, recvs, device):
        pltpu.make_async_remote_copy(
            src_ref=source,
            dst_ref=target,
            send_sem=sends,
            recv_sem=recvs,
            device_id=device,
            device_id_type=MESH,
        ).start()

    def wait_bytes(ref, sem):
        pltpu.make_async_copy(ref, ref, sem).wait()

    def line_gather(slots, sems):
        def send(step):
            device = line_device((line + step) % n_line)
            start_copy(slots.at[line], slots.at[line], sems.at[0], sems.at[1], device)

        repeat(1, n_line, send)

    def plane_scatter(sources, slots, sems):
        def send(step):
            other = (spot + step) % n_plane
            start_copy(
                sources.at[other], slots.at[spot], sems.at[0], sems.at[1], plane_device(other)
            )

        repeat(1, n_plane, send)

    def wait_line(slots, sems, which):
        if n_line > 1:
            wait_bytes(slots.at[pl.ds(0, n_line - 1)], sems.at[which])

    def wait_plane(slots, sems, which):
        if n_plane > 1:
            wait_bytes(slots.at[pl.ds(0, n_plane - 1)], sems.at[which])

    def tile_of(sums, rows):
        rest = jnp.zeros((rows - len(sums), columns), F32)
        return jnp.concatenate(list(sums) + [rest], axis=0)

    def turn(chunk):
        start = chunk * LANES
        if not isinstance(start, int):
            start = pl.multiple_of(start, LANES)
        turned = coarse_ref[:, pl.ds(start, LANES)].astype(F32).T
        count = LANES // width
        coarse_t[pl.ds(chunk * count, count)] = turned.reshape(count, width, width)

    def arrange(member):
        parts = []
        for other_line in range(n_line):
            parts.append(coarse_t[map_ref[other_line * n_plane + member]])
        pieces[member] = jnp.concatenate(parts, axis=0).T.astype(BF16)

    def make_packs(exchange, rounded):
        packs[exchange] = (
            dot(select[...].reshape(-1, owned), rounded)
            .astype(BF16)
            .reshape(packs.shape[1:])
        )

    def send_faces(sources, targets, sends, recvs):
        for face, (device, present, block) in enumerate(faces):

            @pl.when(present)
            def _():
                start_copy(
                    sources[face], targets.at[block], sends.at[face], recvs.at[block], device
                )

    def wait_faces(targets, sems):
        for face, (_, present, _) in enumerate(faces):

            @pl.when(present)
            def _():
                wait_bytes(targets.at[face], sems.at[face])

    def send_packs(exchange):
        send_faces(
            [packs.at[exchange, face] for face in range(4)],
            margins.at[exchange],
            margin_send.at[exchange],
            margin_recv.at[exchange],
        )

    def wait_margins(exchange):
        wait_faces(margins.at[exchange], margin_recv.at[exchange])

    def packed(sums):
        high = sums.astype(BF16).astype(F32)
        middle = (sums - high).astype(BF16).astype(F32)
        low = sums - high - middle
        return jnp.concatenate([high, middle, low, jnp.zeros_like(low)], axis=0).astype(BF16)

    def unpacked(rows):
        return rows[0:4] + rows[4:8] + rows[8:12]

    def store_line(which, parts, sums):
        gathered[which, line, :width, :] = joined(dot(basis_t[...], parts)).astype(BF16)
        gathered[which, line, width:, :] = packed(tile_of(sums, 4))

    def send_line(which):
        line_gather(gathered.at[which], gather_sem.at[which])

    def fold_basis():
        wait_faces(basis_margins, basis_recv)
        folds = []
        for face in range(4):
            folds.append(
                sum(
                    lax.dot_general(
                        spread[part, face],
                        basis_margins[face],
                        (((1,), (1,)), ((), ())),
                        preferred_element_type=F32,
                    )
                    for part in range(2)
                )
            )
        fold[...] = halves(jnp.concatenate(folds, axis=1))

    def apply_both(which, parts):
        local = joined(dot(inverse_ref[:, :owned], parts))
        wait_line(gathered.at[which], gather_sem.at[which], 1)
        products = dot(
            solver[...].reshape(n_plane * width, n_line * width),
            gathered[which, :, :width, :].reshape(n_line * width, columns),
        ).reshape(n_plane, width, columns)
        partial[which, :, :width, :] = products.astype(BF16)
        line_total = packed(
            unpacked(jnp.sum(gathered[which, :, width:, :].astype(F32), axis=0))
        )
        for member in range(n_plane):
            partial[which, member, width:, :] = line_total
        plane_scatter(partial.at[which], received.at[which], partial_sem.at[which])
        received[which, spot] = partial[which, spot]
        wait_margins(2 * which)
        local += dot(inverse_ref[:, owned:], margins[2 * which].reshape(-1, columns))
        make_packs(2 * which + 1, local.astype(BF16))
        send_packs(2 * which + 1)
        if which == 0:
            fold_basis()
        wait_plane(received.at[which], partial_sem.at[which], 1)
        total = jnp.sum(received[which].astype(F32), axis=0)
        solved[which] = total[:width].astype(BF16)
        send_faces(
            [solved.at[which]] * 4,
            solved_margins.at[which],
            solved_send.at[which],
            solved_recv.at[which],
        )
        applied = local + joined(dot(basis_ref[...], halves(total[:width])))
        halved = halves(applied)
        size = block_ref.shape[1]
        own = [
            joined(dot(block_ref[block], halved[block * size : (block + 1) * size]))
            for block in range(block_ref.shape[0])
        ]
        own = own[0] if len(own) == 1 else jnp.concatenate(own, axis=0)
        wait_margins(2 * which + 1)
        for face in range(4):
            margin = margins[2 * which + 1, face]
            own -= dot(spread[0, face], margin) + dot(spread[1, face], margin)
        wait_faces(solved_margins.at[which], solved_recv.at[which])
        coarse = solved_margins[which].reshape(4 * width, columns)
        own -= dot(fold[...], jnp.concatenate([coarse, coarse], axis=0))
        return applied, own, unpacked(total[width:])

    operands["rhs"].wait()
    operands["basis"].wait()
    right_side = rhs_ref[...]
    parts = halves(right_side)
    store_line(0, parts, [column_sum(right_side * right_side)])
    operands["coarse"].wait()
    operands["map"].wait()
    repeat(0, coarse_ref.shape[1] // LANES, turn)
    repeat(0, n_plane, arrange)
    pl.semaphore_wait(barrier, peers)
    send_line(0)
    plane_scatter(pieces, solver, pieces_sem)
    solver[spot] = pieces[spot]
    operands["rows"].wait()
    operands["weight"].wait()
    row_ids = lax.broadcasted_iota(jnp.int32, (owned, rows_ref.shape[1]), 0)
    for face in range(4):
        hit = row_ids == rows_ref[face : face + 1, :]
        one_hot = jnp.where(hit, 1.0, 0.0).astype(F32)
        select[face] = one_hot.T.astype(BF16)
        basis_packs[face] = dot(basis_t[...], one_hot.astype(BF16)).astype(BF16)
    make_packs(0, right_side.astype(BF16))
    send_packs(0)
    send_faces(
        [basis_packs.at[face] for face in range(4)], basis_margins, basis_send, basis_recv
    )
    for face in range(4):
        hit = row_ids == rows_ref[face : face + 1, :]
        weights = jnp.where(hit, weight_ref[face : face + 1, :], 0.0)
        high = weights.astype(BF16)
        spread[0, face] = high
        spread[1, face] = (weights - high.astype(F32)).astype(BF16)
    basis_ref[...] = basis_t[...].astype(F32).T.astype(BF16)
    operands["inverse"].wait()
    operands["block"].wait()
    wait_plane(solver, pieces_sem, 1)

    applied, image, sums = apply_both(0, parts)
    rhs_square = sums[0:1]
    beta = jnp.sqrt(rhs_square + EPSILON)
    one_one = rhs_square / (rhs_square + EPSILON)
    krylov_one = right_side / beta
    image_one = image / beta

    parts = halves(image_one)
    store_line(
        1, parts, [column_sum(image_one * krylov_one), column_sum(image_one * image_one)]
    )
    send_line(1)
    make_packs(2, image_one.astype(BF16))
    send_packs(2)
    precond_one = applied / beta
    applied, image, sums = apply_both(1, parts)
    first_dot, image_square = sums[0:1], sums[1:2]
    remainder_square = image_square + first_dot * first_dot * (one_one - 2.0)
    remainder_square = jnp.maximum(remainder_square, 0.0)
    first_norm = jnp.sqrt(remainder_square + EPSILON)
    precond_two = (applied - first_dot * precond_one) / first_norm

    krylov_two = (image_one - first_dot * krylov_one) / first_norm
    one_two = first_dot * (1.0 - one_one) / first_norm
    two_two = remainder_square / (remainder_square + EPSILON)
    image = (image - first_dot * image_one) / first_norm
    all_sums[place] = tile_of(
        [
            column_sum(image * krylov_one),
            column_sum(image * krylov_two),
            column_sum(image * image),
        ],
        4,
    )

    def send_sums(step):
        start_copy(
            all_sums.at[place], all_sums.at[place], all_sem.at[0], all_sem.at[1], other_device(step)
        )

    repeat(1, n_all, send_sums, 32)
    wait_bytes(all_sums.at[pl.ds(0, n_all - 1)], all_sem.at[1])
    sums = jnp.sum(all_sums[...], axis=0)
    cross_dot, second_dot, image_square = sums[0:1], sums[1:2], sums[2:3]
    remainder_square = (
        image_square
        + cross_dot * cross_dot * (one_one - 2.0)
        + second_dot * second_dot * (two_two - 2.0)
        + 2.0 * cross_dot * second_dot * one_two
    )
    second_norm = jnp.sqrt(jnp.maximum(remainder_square, 0.0) + EPSILON)
    weight_one, weight_two, relative = least_squares(
        beta, first_dot, first_norm, cross_dot, second_dot, second_norm
    )
    out_ref[...] = weight_one * precond_one + weight_two * precond_two
    relative_ref[...] = relative

    wait_bytes(all_sums.at[pl.ds(0, n_all - 1)], all_sem.at[0])
    wait_plane(solver, pieces_sem, 0)
    for which in range(2):
        wait_line(gathered.at[which], gather_sem.at[which], 0)
        wait_plane(received.at[which], partial_sem.at[which], 0)
    for exchange in range(4):
        for face, (_, present, _) in enumerate(faces):

            @pl.when(present)
            def _():
                wait_bytes(packs.at[exchange, face], margin_send.at[exchange, face])

    wait_faces(basis_packs, basis_send)
    for which in range(2):
        wait_faces(solved_margins.at[which], solved_send.at[which])


def on_device(
    n_gx,
    n_gy,
    rhs,
    face_rows,
    margin_weight,
    local_blocks,
    subdomain_inverse,
    coarse_basis,
    coarse_inverse,
    coarse_map,
):
    plane = 4 if n_gx % 4 == 0 else 1
    n_line, n_plane = n_gx // plane, plane * n_gy
    owned, columns = rhs.shape[2:]
    margin_rows = face_rows.shape[3]
    width = coarse_basis.shape[3]
    n_coarse = coarse_inverse.shape[3]
    vmem = pl.BlockSpec(memory_space=pltpu.VMEM)
    operands = (
        rhs[0, 0],
        face_rows[0, 0],
        margin_weight[0, 0],
        local_blocks[0, 0],
        subdomain_inverse[0, 0],
        coarse_basis[0, 0].T,
        coarse_inverse[0, 0],
        coarse_map,
    )
    dma = pltpu.SemaphoreType.DMA
    result, relative = pl.pallas_call(
        functools.partial(kernel, n_gx, n_gy, plane),
        out_shape=(
            jax.ShapeDtypeStruct((owned, columns), F32),
            jax.ShapeDtypeStruct((1, columns), F32),
        ),
        in_specs=[pl.BlockSpec(memory_space=pl.ANY)] * len(operands),
        out_specs=(vmem, vmem),
        scratch_shapes=[pltpu.VMEM(each.shape, each.dtype) for each in operands[:-1]]
        + [
            pltpu.SMEM(coarse_map.shape, coarse_map.dtype),
            pltpu.VMEM((n_coarse // width, width, width), F32),
            pltpu.VMEM((n_plane, width, n_line * width), BF16),
            pltpu.VMEM((n_plane, width, n_line * width), BF16),
            pltpu.VMEM((4, margin_rows, owned), BF16),
            pltpu.VMEM((2, 4, owned, margin_rows), BF16),
            pltpu.VMEM((owned, width), BF16),
            pltpu.VMEM((4, 4, margin_rows, columns), BF16),
            pltpu.VMEM((4, 4, margin_rows, columns), BF16),
            pltpu.VMEM((2, n_line, width + 16, columns), BF16),
            pltpu.VMEM((2, n_plane, width + 16, columns), BF16),
            pltpu.VMEM((2, n_plane, width + 16, columns), BF16),
            pltpu.VMEM((n_gx * n_gy, 4, columns), F32),
            pltpu.VMEM((4, width, margin_rows), BF16),
            pltpu.VMEM((4, width, margin_rows), BF16),
            pltpu.VMEM((owned, 8 * width), BF16),
            pltpu.VMEM((2, width, columns), BF16),
            pltpu.VMEM((2, 4, width, columns), BF16),
            dma((len(operands),)),
            dma((4,)),
            dma((4,)),
            dma((2, 4)),
            dma((2, 4)),
            dma((2,)),
            dma((4, 4)),
            dma((4, 4)),
            dma((2, 2)),
            dma((2, 2)),
            dma((2,)),
        ],
        compiler_params=pltpu.CompilerParams(
            collective_id=0, has_side_effects=True, vmem_limit_bytes=56 * 1024 * 1024
        ),
    )(*operands)
    return (result[None, None], relative[0])


def solution(mesh):
    return jax.shard_map(
        functools.partial(on_device, mesh.shape["gx"], mesh.shape["gy"]),
        mesh=mesh,
        in_specs=(
            P("gx", "gy", None, None),
            P("gx", "gy", None, None),
            P("gx", "gy", None, None),
            P("gx", "gy", None, None, None),
            P("gx", "gy", None, None),
            P("gx", "gy", None, None),
            P("gx", "gy", None, None),
            P(),
        ),
        out_specs=(P("gx", "gy", None, None), P()),
        check_vma=False,
    )
```
